32 devices in a mesh: dp: 4 (over z), ctx: 2 (over x), tensor: 4 (over y, core).
Axes of the slice: x: 2, y: 2, z: 4, core: 2. Of those that a mesh axis runs over, the one named last changes fastest.
Arguments:
- tokens: bfloat16 [2, 4, 512, 2048], P(None, 'dp', 'ctx'), may hold values from -6 to 6
- doc_lengths: int32 [2, 4, 6], P(None, 'dp'), may hold values from 1 to 384, as said below
- w_query: bfloat16 [2, 2048, 1280], P(None, ('dp', 'ctx'), 'tensor'), may hold values from -0.125 to 0.125
- w_key: bfloat16 [2, 2048, 320], P(None, ('dp', 'ctx')), may hold values from -0.125 to 0.125
- w_value: bfloat16 [2, 2048, 320], P(None, ('dp', 'ctx')), may hold values from -0.125 to 0.125
- w_out: bfloat16 [2, 1280, 2048], P(None, 'tensor', ('dp', 'ctx')), may hold values from -0.625 to 0.625
- w_gate: bfloat16 [2, 2048, 5120], P(None, ('dp', 'ctx'), 'tensor'), may hold values from -0.125 to 0.125
- w_up: bfloat16 [2, 2048, 5120], P(None, ('dp', 'ctx'), 'tensor'), may hold values from -0.125 to 0.125
- w_down: bfloat16 [2, 5120, 2048], P(None, 'tensor', ('dp', 'ctx')), may hold values from -0.078125 to 0.078125
- norm_gains: bfloat16 [2, 4224], P(None, ('dp', 'ctx')), may hold values from 0.25 to 1.75
- cotangent: bfloat16 [2, 4, 512, 2048], P(None, 'dp', 'ctx'), may hold values from -6 to 6
Outputs:
- output: bfloat16 [2, 4, 512, 2048], P(None, 'dp', 'ctx')
- grad_input: float32 [2, 4, 512, 2048], P(None, 'dp', 'ctx')
- grad_query: float32 [2, 2048, 1280], P(None, ('dp', 'ctx'), 'tensor')
- grad_key: float32 [2, 2048, 320], P(None, ('dp', 'ctx'))
- grad_value: float32 [2, 2048, 320], P(None, ('dp', 'ctx'))
- grad_out: float32 [2, 1280, 2048], P(None, 'tensor', ('dp', 'ctx'))
- grad_gate: float32 [2, 2048, 5120], P(None, ('dp', 'ctx'), 'tensor')
- grad_up: float32 [2, 2048, 5120], P(None, ('dp', 'ctx'), 'tensor')
- grad_down: float32 [2, 5120, 2048], P(None, 'tensor', ('dp', 'ctx'))
- grad_gains: float32 [2, 4224], P(None, ('dp', 'ctx'))
The draws below stay inside these ranges and needn't reach their ends.
Inputs may be any that keep to these rules, and one draw needn't show every extreme that they name: `doc_lengths`: each sequence holds 6 documents from its start, followed by padding of one token or more. One document of each sequence, at a place drawn from the seed, is exactly 384 tokens long.
All inputs are finite; a program needn't handle non-finite values.
Results may differ from the reference program's by a relative error of at most 0.034.
Values may be sent and summed in bfloat16 or wider, within the bound.
A program may use at most 320 MiB of HBM per device.

```python
import jax
import jax.numpy as jnp
from jax import lax

D = 2048
HQ = 20
HK = 5
HD = 64
FF = 5120
LENGTH = 512
DOCS = 6
MICRO = 2
LAYERS = 2
SEQUENCES = 4
N_TENSOR = 4


def draw_doc_lengths(key, part):
    key = jax.random.fold_in(key, 7)
    first_key, second_key, place_key = jax.random.split(key, 3)
    shape = (MICRO, SEQUENCES, DOCS)
    upper = LENGTH // (4 * DOCS)
    first_factor = jax.random.randint(first_key, shape, 0, upper + 1)
    second_factor = jax.random.randint(second_key, shape, 0, upper + 1)
    small_docs = 1 + first_factor * second_factor // upper
    big_place = jax.random.randint(place_key, (MICRO, SEQUENCES, 1), 0, DOCS)
    members = jnp.arange(DOCS, dtype=jnp.int32)
    return jnp.where(members == big_place, LENGTH // 2 + LENGTH // 4, small_docs).astype(jnp.int32)


def spiked(array, own_key, source, target, blocks, factor):
    owner, partner = [(jnp.arange(array.shape[dim]) // (array.shape[dim] // blocks)).reshape([-1 if axis == dim else 1 for axis in range(array.ndim)]) for dim in (source, target)]
    chosen = jax.random.permutation(own_key, blocks)[partner]
    strong = (owner == chosen) | (owner == (partner + blocks // 2) % blocks)
    return jnp.where(strong, factor * array, array)


def shard_levels(key, shape, pieces, least, high):
    loudness, own = 1.0, jax.random.fold_in(key, 6)
    for dim, shards_of in pieces:
        heights = jnp.exp(jax.random.uniform(jax.random.fold_in(own, dim), (shards_of,), jnp.float32, least / len(pieces), high / len(pieces)))
        loudness = loudness * jnp.repeat(heights, shape[dim] // shards_of).reshape([-1 if axis == dim else 1 for axis in range(len(shape))])
    return loudness


def normal_values(key, shape, width, bound, shards=(), kind=jnp.bfloat16):
    level = shard_levels(key, shape, shards, -0.22, 0.18) if shards else 1.0
    values = jax.random.normal(key, shape, jnp.float32) * width * level
    return jnp.minimum(jnp.maximum(values, -bound), bound).astype(kind)


def bell_draw_with(stream_key, shape, scale, most, cuts, heavy, kind=jnp.bfloat16):
    array = scale * jax.random.normal(stream_key, shape, jnp.float32)
    if cuts:
        array = array * shard_levels(stream_key, shape, cuts, -0.22, 0.18)
    return jnp.clip(spiked(array, jax.random.fold_in(stream_key, 3), *heavy), -most, most).astype(kind)


def setup_inputs(seed: int = 0) -> dict:
    key_of = jax.random.split(jax.random.key(seed), 12)
    tokens = normal_values(key_of[0], (MICRO, SEQUENCES, LENGTH, D), 1.0, 6.0, ((1, 4), (2, 2)))
    doc_lengths = draw_doc_lengths(jax.random.fold_in(key_of[11], 71), 0)
    w_query = normal_values(key_of[2], (LAYERS, D, HQ * HD), D ** -0.5, 0.125, ((1, 8), (2, 4)))
    w_key = normal_values(key_of[3], (LAYERS, D, HK * HD), D ** -0.5, 0.125, ((1, 8),))
    w_value = normal_values(key_of[4], (LAYERS, D, HK * HD), D ** -0.5, 0.125, ((1, 8),))
    w_out = normal_values(key_of[5], (LAYERS, HQ * HD, D), (HQ * HD // 16) ** -0.5, 0.625, ((1, 4), (2, 8)))
    w_gate = normal_values(key_of[6], (LAYERS, D, FF), D ** -0.5, 0.125, ((1, 8), (2, 4)))
    w_up = normal_values(key_of[7], (LAYERS, D, FF), D ** -0.5, 0.125, ((1, 8), (2, 4)))
    w_down = normal_values(key_of[8], (LAYERS, FF, D), FF ** -0.5, 0.078125, ((1, 4), (2, 8)))
    norm_gains = jnp.clip(1.0 + 0.15 * jax.random.normal(key_of[9], (LAYERS, 2 * D + 2 * HD), jnp.float32), 0.25, 1.75).astype(jnp.bfloat16)
    cotangent = bell_draw_with(key_of[10], (MICRO, SEQUENCES, LENGTH, D), 1.0, 6.0, ((1, 4), (2, 2)), (1, 3, 4, 2.0))
    return dict(tokens=tokens, doc_lengths=doc_lengths, w_query=w_query, w_key=w_key, w_value=w_value, w_out=w_out, w_gate=w_gate, w_up=w_up, w_down=w_down, norm_gains=norm_gains, cotangent=cotangent)


epsilon = 1e-05
rope_base = 10000.0

@jax.custom_vjp
def low(v):
    return lax.optimization_barrier(v.astype(jnp.bfloat16)).astype(jnp.float32)

@jax.custom_vjp
def low_back(v):
    return v

def low_keep(v):
    return (low(v), None)

def low_pass(kept, grad):
    return (grad,)

def back_keep(v):
    return (v, None)

def back_low(kept, grad):
    return (low(grad),)
low.defvjp(low_keep, low_pass)
low_back.defvjp(back_keep, back_low)

def layout(doc_lengths, length):
    ends = jnp.cumsum(doc_lengths, axis=-1, dtype=jnp.int32)
    starts = ends - doc_lengths
    places = jnp.arange(length, dtype=jnp.int32)
    document = lax.optimization_barrier(jnp.sum((places[:, None] >= ends[..., None, :]).astype(jnp.int32), axis=-1, dtype=jnp.int32))
    chosen = document[..., None] == jnp.arange(doc_lengths.shape[-1], dtype=jnp.int32)
    begins = lax.optimization_barrier(jnp.sum(jnp.where(chosen, starts[..., None, :], 0), axis=-1, dtype=jnp.int32))
    segment = jnp.where(document < doc_lengths.shape[-1], document, -1)
    return (segment, places - begins)

def rotation(position):
    half_size = HD // 2
    frequency = rope_base ** (-jnp.arange(half_size, dtype=jnp.float32) * (2.0 / HD))
    angle = position.astype(jnp.float32)[..., None, None] * frequency
    return (jnp.cos(angle), jnp.sin(angle))

def rotate(values, cosine, sine_value):
    half_size = values.shape[-1] // 2
    first_half = values[..., :half_size]
    second_half = values[..., half_size:]
    return jnp.concatenate([first_half * cosine - second_half * sine_value, second_half * cosine + first_half * sine_value], axis=-1)

def rms_norm(values, gain_vector):
    return values * lax.rsqrt(lax.optimization_barrier(jnp.mean(values * values, axis=-1, keepdims=True)) + epsilon) * gain_vector

def dense(left_side, right_side):
    return jnp.dot(left_side, right_side, precision=lax.Precision.HIGHEST)

def attend(inputs):
    queries, key_heads, value_heads, segment = inputs
    places = jnp.arange(segment.shape[0], dtype=jnp.int32)
    allowed = (segment[:, None] == segment[None, :]) & (segment[:, None] >= 0) & (places[None, :] <= places[:, None])
    scores = jnp.einsum('qhd,khd->hqk', queries, key_heads, precision=lax.Precision.HIGHEST) * HD ** (-0.5)
    scores = low_back(scores)
    masked = jnp.where(allowed[None], scores, -1e+30)
    highest = lax.optimization_barrier(jnp.max(masked, axis=-1, keepdims=True))
    exponent = jnp.where(allowed[None], jnp.exp(masked - highest), 0.0)
    row_total = lax.optimization_barrier(jnp.sum(exponent, axis=-1, keepdims=True))
    probability = low(exponent / jnp.where(row_total > 0.0, row_total, 1.0))
    return jnp.einsum('hqk,khd->qhd', probability, value_heads, precision=lax.Precision.HIGHEST)

def block(state, weights, segment, cosine, sine_value):
    w_q, w_k, w_v, w_o, w_g, w_u, w_d, gain_all = weights
    g_attn = gain_all[:D]
    g_ffn = gain_all[D:2 * D]
    g_query = gain_all[2 * D:2 * D + HD]
    g_key = gain_all[2 * D + HD:]
    per_group = HQ // N_TENSOR
    group_size = HQ // HK
    span_units = FF // N_TENSOR
    sequences, length = (state.shape[0], state.shape[1])
    normed = low(rms_norm(state, g_attn))
    attn = jnp.zeros_like(state)
    for group in range(N_TENSOR):
        first_head = group * per_group
        first_pair = first_head // group_size
        pair_count = (first_head + per_group - 1) // group_size - first_pair + 1
        used = low_back(normed)
        queries = low_back(dense(used, w_q[:, first_head * HD:(first_head + per_group) * HD]))
        queries = queries.reshape(sequences, length, per_group, HD)
        queries = low(rotate(rms_norm(queries, g_query), cosine, sine_value))
        key_rows = low_back(dense(used, w_k[:, first_pair * HD:(first_pair + pair_count) * HD]))
        key_rows = key_rows.reshape(sequences, length, pair_count, HD)
        key_rows = low(rotate(rms_norm(key_rows, g_key), cosine, sine_value))
        value_rows = low(low_back(dense(used, w_v[:, first_pair * HD:(first_pair + pair_count) * HD])))
        value_rows = value_rows.reshape(sequences, length, pair_count, HD)
        chosen = jnp.asarray([(first_head + member) // group_size - first_pair for member in range(per_group)], dtype=jnp.int32)
        key_heads = jnp.take(key_rows, chosen, axis=2)
        value_heads = jnp.take(value_rows, chosen, axis=2)
        mixed = lax.map(jax.checkpoint(attend), (queries, key_heads, value_heads, segment))
        mixed = low(low_back(mixed.reshape(sequences, length, per_group * HD)))
        attn = attn + low(dense(mixed, w_o[first_head * HD:(first_head + per_group) * HD]))
    middle = state + low_back(attn)
    normed2 = low(rms_norm(middle, g_ffn))
    ffn = jnp.zeros_like(state)
    for group in range(N_TENSOR):
        used = low_back(normed2)
        gate_value = low_back(dense(used, w_g[:, group * span_units:(group + 1) * span_units]))
        up_value = low_back(dense(used, w_u[:, group * span_units:(group + 1) * span_units]))
        hidden = low(jax.nn.silu(gate_value) * up_value)
        ffn = ffn + low(dense(hidden, w_d[group * span_units:(group + 1) * span_units]))
    return middle + low_back(ffn)

def reference(tokens, doc_lengths, w_query, w_key, w_value, w_out, w_gate, w_up, w_down, norm_gains, cotangent):
    micro_count, sequences, length, model_width = tokens.shape
    segment, position = layout(doc_lengths, length)
    segment = segment.reshape(micro_count * sequences, length)
    cosine, sine_value = rotation(position.reshape(micro_count * sequences, length))
    weights = (w_query.astype(jnp.float32), w_key.astype(jnp.float32), w_value.astype(jnp.float32), w_out.astype(jnp.float32), w_gate.astype(jnp.float32), w_up.astype(jnp.float32), w_down.astype(jnp.float32), norm_gains.astype(jnp.float32))

    def forward(state, *layer_weights):
        for layer_index in range(LAYERS):
            state = block(state, tuple((weight[layer_index] for weight in layer_weights)), segment, cosine, sine_value)
        return state
    start = tokens.astype(jnp.float32).reshape(micro_count * sequences, length, model_width)
    final, pull = jax.vjp(forward, start, *weights)
    live_rows = (segment >= 0).astype(jnp.float32)[..., None]
    start_grad = cotangent.astype(jnp.float32).reshape(micro_count * sequences, length, model_width) * live_rows
    grads = pull(start_grad)
    return (final.astype(jnp.bfloat16).reshape(tokens.shape), grads[0].reshape(tokens.shape), grads[1], grads[2], grads[3], grads[4], grads[5], grads[6], grads[7], grads[8])
```

```python
import jax
import jax.numpy as jnp
from jax import lax
from jax.sharding import PartitionSpec as P

HQ = 20
HK = 5
HD = 64
LAYERS = 2
GROUP_SIZE = HQ // HK

epsilon = 1e-05
rope_base = 10000.0

f32 = jnp.float32
bf16 = jnp.bfloat16


def product(left_side, right_side, contract):
    return lax.dot_general(
        left_side, right_side, (contract, ((), ())), preferred_element_type=f32
    )


def rotate(values, cosine, sine_value):
    half_size = values.shape[-1] // 2
    first_half = values[..., :half_size]
    second_half = values[..., half_size:]
    return jnp.concatenate(
        [
            first_half * cosine - second_half * sine_value,
            second_half * cosine + first_half * sine_value,
        ],
        axis=-1,
    )


def scale_of(values):
    return lax.rsqrt(jnp.mean(values * values, axis=-1, keepdims=True) + epsilon)


def norm_back(gradient, values, scaling, gain_vector):
    scaled = gradient * gain_vector
    cubed = scaling * scaling * scaling
    return scaling * scaled - values * cubed * jnp.mean(scaled * values, axis=-1, keepdims=True)


class Plan:
    def __init__(self):
        self.n = lax.axis_size("dp")
        self.nt = lax.axis_size("tensor")
        assert lax.axis_size("ctx") == 2 and self.nt == 4
        self.z = lax.axis_index("dp")
        self.x = lax.axis_index("ctx")
        self.t = lax.axis_index("tensor")
        self.y = self.t // 2
        self.c = self.t % 2
        nt = self.nt
        places = [(a, b, d) for a in range(2) for b in range(2) for d in range(2)]
        self.peers = {}
        for j in range(1, 4):
            self.peers[j] = [
                (a * nt + 2 * b + d, (a ^ (j // 2)) * nt + 2 * (b ^ (j % 2)) + d)
                for a, b, d in places
            ]
        self.swap_pairs = [(a * nt + 2 * b + d, d * nt + 2 * b + a) for a, b, d in places]
        self.core_pairs = [(i, i ^ 1) for i in range(nt)]
        self.up = [(i, (i + 1) % self.n) for i in range(self.n)]
        self.down = [(i, (i - 1) % self.n) for i in range(self.n)]

    def peer(self, value, j):
        return lax.ppermute(value, ("ctx", "tensor"), self.peers[j])

    def swap(self, value):
        return lax.ppermute(value, ("ctx", "tensor"), self.swap_pairs)

    def core(self, value):
        return lax.ppermute(value, "tensor", self.core_pairs)

    def fetch(self, shard):
        own = [self.swap(shard)]
        for _ in range(1, self.n):
            own.append(lax.ppermute(own[-1], "dp", self.down))
        other = [self.core(piece) for piece in own]
        return jnp.concatenate(own + other, axis=0)

    def scatter(self, grad):
        half = grad.shape[0] // 2
        w = half // self.n
        both = grad[:half].astype(f32) + self.core(grad[half:]).astype(f32)
        total = both[(self.n - 1) * w :]
        for s in reversed(range(self.n - 1)):
            moved = lax.ppermute(total.astype(bf16), "dp", self.up)
            total = both[s * w : (s + 1) * w] + moved.astype(f32)
        return self.swap(total.astype(bf16))

    def spread(self, rows):
        return jnp.concatenate([rows] + [self.peer(rows, j) for j in range(1, 4)], axis=0)

    def gather_sum(self, terms):
        rows = terms.shape[0] // 4
        total = terms[:rows].astype(f32)
        for j in range(1, 4):
            total = total + self.peer(terms[j * rows : (j + 1) * rows], j).astype(f32)
        return total

    def inward(self, array):
        lead = array.shape[:-1]
        d = array.shape[-1]
        w = d // (2 * self.n)
        parts = array.reshape(lead + (self.n, 2, w))
        axis = len(lead)
        twice = jnp.concatenate([parts, parts], axis=axis)
        rolled = lax.dynamic_slice_in_dim(twice, self.z, self.n, axis=axis)
        rolled = jnp.where(self.c == 0, rolled, jnp.flip(rolled, axis + 1))
        return jnp.swapaxes(rolled, axis, axis + 1).reshape(lead + (d,))

    def outward(self, array):
        lead = array.shape[:-1]
        d = array.shape[-1]
        w = d // (2 * self.n)
        axis = len(lead)
        parts = jnp.swapaxes(array.reshape(lead + (2, self.n, w)), axis, axis + 1)
        parts = jnp.where(self.c == 0, parts, jnp.flip(parts, axis + 1))
        twice = jnp.concatenate([parts, parts], axis=axis)
        rolled = lax.dynamic_slice_in_dim(twice, (self.n - self.z) % self.n, self.n, axis=axis)
        return rolled.reshape(lead + (d,))

    def replicate(self, rows):
        beside = self.peer(rows, 1)
        half = jnp.where(
            self.y == 0,
            jnp.concatenate([rows, beside], axis=0),
            jnp.concatenate([beside, rows], axis=0),
        )
        other = self.core(half)
        return jnp.where(self.c == 0, jnp.stack([half, other]), jnp.stack([other, half]))


def pairs_of(rows, first_pair):
    return jnp.where(first_pair[:, None, None], rows[None, :, 0], rows[None, :, 1])


def attend(queries, key_heads, value_heads, allowed):
    scores = (
        jnp.einsum("hqd,hkd->hqk", queries, key_heads, preferred_element_type=f32) * HD ** (-0.5)
    )
    masked = jnp.where(allowed, scores, -1e30)
    highest = jnp.max(masked, axis=-1, keepdims=True)
    exponent = jnp.where(allowed, jnp.exp(masked - highest), 0.0)
    row_total = jnp.sum(exponent, axis=-1, keepdims=True)
    live_rows = row_total > 0.0
    safe_total = jnp.where(live_rows, row_total, 1.0)
    probability = (exponent / safe_total).astype(bf16)
    mixed = jnp.einsum("hqk,hkd->hqd", probability, value_heads, preferred_element_type=f32)
    merged = jnp.where(live_rows, highest + jnp.log(safe_total), 0.0)
    return mixed, merged


def attend_back(queries, key_heads, value_heads, grad_mixed, merged, allowed):
    scores = (
        jnp.einsum("hqd,hkd->hqk", queries, key_heads, preferred_element_type=f32) * HD ** (-0.5)
    )
    probability = jnp.where(allowed, jnp.exp(scores - merged), 0.0)
    grad_value_heads = jnp.einsum(
        "hqk,hqd->hkd", probability.astype(bf16), grad_mixed, preferred_element_type=f32
    )
    grad_prob = jnp.einsum("hqd,hkd->hqk", grad_mixed, value_heads, preferred_element_type=f32)
    row_delta = jnp.sum(probability * grad_prob, axis=-1, keepdims=True)
    grad_scores = (probability * (grad_prob - row_delta)).astype(bf16)
    grad_queries = jnp.einsum(
        "hqk,hkd->hqd", grad_scores, key_heads, preferred_element_type=f32
    ) * HD ** (-0.5)
    grad_key_heads = jnp.einsum(
        "hqk,hqd->hkd", grad_scores, queries, preferred_element_type=f32
    ) * HD ** (-0.5)
    return grad_queries, grad_key_heads, grad_value_heads


def local(
    tokens, doc_lengths, w_query, w_key, w_value, w_out, w_gate, w_up, w_down, norm_gains, cotangent
):
    plan = Plan()
    micro_count, sequences, half_rows, width = tokens.shape
    assert micro_count == 2 and sequences == 1
    quarter = half_rows // 2
    heads = w_query.shape[2] // HD
    n = plan.n
    group = 2 * plan.y + plan.x
    qw, kw = heads * HD, 2 * HD

    kv_at = plan.t * heads // GROUP_SIZE * HD
    fetched = []
    for layer in range(LAYERS):
        keys = lax.dynamic_slice_in_dim(w_key[layer], kv_at, kw, axis=1)
        values = lax.dynamic_slice_in_dim(w_value[layer], kv_at, kw, axis=1)
        attn_shard = jnp.concatenate([w_query[layer], keys, values, w_out[layer].T], axis=1)
        attn_w = plan.fetch(attn_shard)
        fetched.append(
            (
                attn_w[:, : qw + 2 * kw],
                attn_w[:, qw + 2 * kw :],
                plan.fetch(w_gate[layer]),
                plan.fetch(w_up[layer]),
                plan.fetch(w_down[layer].T),
            )
        )

    side = lax.ppermute(norm_gains, "ctx", [(0, 1), (1, 0)])
    pair = jnp.where(
        plan.x == 0,
        jnp.concatenate([norm_gains, side], axis=1),
        jnp.concatenate([side, norm_gains], axis=1),
    )
    gain_pieces = [pair]
    for _ in range(1, n):
        gain_pieces.append(lax.ppermute(gain_pieces[-1], "dp", plan.down))
    ring = jnp.concatenate(gain_pieces + gain_pieces, axis=1)
    gain_width = pair.shape[1]
    gains = lax.dynamic_slice_in_dim(
        ring, (n - plan.z) % n * gain_width, n * gain_width, axis=1
    ).astype(f32)
    gain_attn = plan.inward(gains[:, :width])
    gain_ffn = plan.inward(gains[:, width : 2 * width])
    gain_query = gains[:, 2 * width : 2 * width + HD]
    gain_key = gains[:, 2 * width + HD :]

    blocks = jnp.arange(4, dtype=jnp.int32) ^ (2 * plan.x + plan.y).astype(jnp.int32)
    places = (blocks[:, None] * quarter + jnp.arange(quarter, dtype=jnp.int32)[None, :]).reshape(-1)
    lengths = lax.dynamic_index_in_dim(doc_lengths, plan.c, axis=0, keepdims=False)[0]
    docs = lengths.shape[0]
    ends = jnp.cumsum(lengths, dtype=jnp.int32)
    starts = ends - lengths
    document = jnp.sum((places[:, None] >= ends[None, :]).astype(jnp.int32), axis=-1)
    chosen = document[:, None] == jnp.arange(docs, dtype=jnp.int32)[None, :]
    position = places - jnp.sum(jnp.where(chosen, starts[None, :], 0), axis=-1)
    segment = jnp.where(document < docs, document, -1)
    allowed = (
        (segment[:, None] == segment[None, :])
        & (segment[:, None] >= 0)
        & (places[None, :] <= places[:, None])
    )[None]
    frequency = rope_base ** (-jnp.arange(HD // 2, dtype=f32) * (2.0 / HD))
    angle = position.astype(f32)[:, None] * frequency
    cosine, sine_value = jnp.cos(angle), jnp.sin(angle)
    pair_start = group * heads // GROUP_SIZE
    first_pair = (
        group * heads + jnp.arange(heads, dtype=jnp.int32)
    ) // GROUP_SIZE == pair_start
    weight_first = first_pair.astype(f32)[:, None, None]

    def own_half(array):
        rows = lax.dynamic_index_in_dim(array, plan.c, axis=0, keepdims=False)[0]
        rows = jnp.where(plan.y == 0, rows, jnp.roll(rows, quarter, axis=0))
        return plan.inward(rows)

    def by_head(array, count):
        return jnp.swapaxes(array.reshape(array.shape[0], count, HD), 0, 1)

    def flat(array):
        return jnp.swapaxes(array, 0, 1).reshape(array.shape[1], -1)

    first_half = own_half(tokens)
    cot_half = own_half(cotangent)
    cot_all = jnp.concatenate([cot_half, plan.peer(cot_half, 2)], axis=0)
    tokens_all = jnp.concatenate([first_half, plan.peer(first_half, 2)], axis=0).astype(f32)
    start_grad = jnp.where(segment[:, None] >= 0, cot_all, jnp.zeros_like(cot_all))

    state = tokens_all[:quarter]
    stored = []
    output = None
    for layer in range(LAYERS):
        w_qkv, w_o, w_g, w_u, w_d = fetched[layer]
        if layer == 0:
            scale_in = scale_of(tokens_all)
            normed = (tokens_all * scale_in * gain_attn[layer]).astype(bf16)
            scale_in = scale_in[:quarter]
        else:
            scale_in = scale_of(state)
            normed = plan.spread((state * scale_in * gain_attn[layer]).astype(bf16))
        qkv = product(normed, w_qkv, ((1,), (0,)))
        queries = by_head(qkv[:, :qw], heads)
        query_scale = scale_of(queries)
        query_low = rotate(queries * query_scale * gain_query[layer], cosine, sine_value).astype(
            bf16
        )
        keys = by_head(qkv[:, qw : qw + kw], 2)
        key_scale = scale_of(keys)
        key_low = rotate(keys * key_scale * gain_key[layer], cosine, sine_value).astype(bf16)
        value_low = by_head(qkv[:, qw + kw :].astype(bf16), 2)
        key_heads = jnp.where(first_pair[:, None, None], key_low[0][None], key_low[1][None])
        value_heads = jnp.where(first_pair[:, None, None], value_low[0][None], value_low[1][None])
        mixed, merged = attend(query_low, key_heads, value_heads, allowed)
        mixed_low = flat(mixed.astype(bf16))
        attn = plan.gather_sum(product(mixed_low, w_o, ((1,), (1,))).astype(bf16))
        middle = state + attn
        scale_mid = scale_of(middle)
        normed2 = plan.spread((middle * scale_mid * gain_ffn[layer]).astype(bf16))
        gate = product(normed2, w_g, ((1,), (0,)))
        up = product(normed2, w_u, ((1,), (0,)))
        hidden = (jax.nn.silu(gate) * up).astype(bf16)
        ffn = plan.gather_sum(product(hidden, w_d, ((1,), (1,))).astype(bf16))
        stored.append(
            (
                state,
                scale_in,
                normed,
                queries,
                query_scale,
                query_low,
                keys,
                key_scale,
                key_heads,
                value_heads,
                merged,
                mixed_low,
                middle,
                scale_mid,
                normed2,
                gate,
                up,
                hidden,
            )
        )
        state = middle + ffn
    output = plan.replicate(plan.outward(state.astype(bf16)))

    gradient = start_grad[:quarter].astype(f32)
    grad_ffn = start_grad
    results = [None] * LAYERS
    gain_grads = [None] * LAYERS
    for layer in reversed(range(LAYERS)):
        w_qkv, w_o, w_g, w_u, w_d = fetched[layer]
        (
            state,
            scale_in,
            normed,
            queries,
            query_scale,
            query_low,
            keys,
            key_scale,
            key_heads,
            value_heads,
            merged,
            mixed_low,
            middle,
            scale_mid,
            normed2,
            gate,
            up,
            hidden,
        ) = stored[layer]
        if grad_ffn is None:
            grad_ffn = plan.spread(gradient.astype(bf16))
        grad_w_d = plan.scatter(product(grad_ffn, hidden, ((0,), (0,))).astype(bf16))
        grad_hidden = product(grad_ffn, w_d, ((1,), (0,)))
        sigmoid_gate = jax.nn.sigmoid(gate)
        grad_gate = (
            grad_hidden * up * sigmoid_gate * (1.0 + gate * (1.0 - sigmoid_gate))
        ).astype(bf16)
        grad_up = (grad_hidden * (gate * sigmoid_gate)).astype(bf16)
        grad_w_g = plan.scatter(product(normed2, grad_gate, ((0,), (0,))).astype(bf16))
        grad_w_u = plan.scatter(product(normed2, grad_up, ((0,), (0,))).astype(bf16))
        term_mid = product(grad_gate, w_g, ((1,), (1,))) + product(grad_up, w_u, ((1,), (1,)))
        summed_mid = plan.gather_sum(term_mid.astype(bf16))
        grad_g_ffn = jnp.sum(summed_mid * middle * scale_mid, axis=0)
        grad_mid = gradient + norm_back(summed_mid, middle, scale_mid, gain_ffn[layer])
        grad_attn = plan.spread(grad_mid.astype(bf16))
        grad_mixed = by_head(product(grad_attn, w_o, ((1,), (0,))).astype(bf16), heads)
        grad_w_o = product(grad_attn, mixed_low, ((0,), (0,))).astype(bf16)
        grad_query_rot, grad_key_heads, grad_value_heads = attend_back(
            query_low, key_heads, value_heads, grad_mixed, merged, allowed
        )
        grad_key_rot = jnp.stack(
            [
                jnp.sum(grad_key_heads * weight_first, axis=0),
                jnp.sum(grad_key_heads * (1.0 - weight_first), axis=0),
            ]
        )
        grad_values = jnp.concatenate(
            [
                jnp.sum(grad_value_heads * weight_first, axis=0),
                jnp.sum(grad_value_heads * (1.0 - weight_first), axis=0),
            ],
            axis=1,
        ).astype(bf16)
        grad_query_norm = rotate(grad_query_rot, cosine, -sine_value)
        grad_g_query = jnp.sum(grad_query_norm * queries * query_scale, axis=(0, 1))
        grad_queries = flat(
            norm_back(grad_query_norm, queries, query_scale, gain_query[layer]).astype(bf16)
        )
        grad_key_norm = rotate(grad_key_rot, cosine, -sine_value)
        grad_g_key = jnp.sum(grad_key_norm * keys * key_scale, axis=(0, 1))
        grad_keys = flat(norm_back(grad_key_norm, keys, key_scale, gain_key[layer]).astype(bf16))
        grad_qkv = jnp.concatenate([grad_queries, grad_keys, grad_values], axis=1)
        grad_w_qkv = product(normed, grad_qkv, ((0,), (0,))).astype(bf16)
        grad_w_attn = plan.scatter(jnp.concatenate([grad_w_qkv, grad_w_o], axis=1))
        summed_in = plan.gather_sum(product(grad_qkv, w_qkv, ((1,), (1,))).astype(bf16))
        grad_g_attn = jnp.sum(summed_in * state * scale_in, axis=0)
        gradient = grad_mid + norm_back(summed_in, state, scale_in, gain_attn[layer])
        grad_ffn = None
        results[layer] = (grad_w_attn, grad_w_g, grad_w_u, grad_w_d)
        gain_grads[layer] = jnp.concatenate(
            [plan.outward(grad_g_attn), plan.outward(grad_g_ffn), grad_g_query, grad_g_key]
        )
    grad_input = plan.replicate(plan.outward(gradient.astype(bf16))).astype(f32)

    def stack(pick):
        return jnp.stack([pick(results[layer]) for layer in range(LAYERS)])

    slice_width = w_query.shape[1]
    shared = jnp.stack(
        [
            jnp.stack(
                [results[layer][0][:, qw : qw + kw], results[layer][0][:, qw + kw : qw + 2 * kw]]
            )
            for layer in range(LAYERS)
        ]
    )
    wide = jnp.zeros(shared.shape[:-1] + (w_key.shape[2],), bf16)
    wide = lax.dynamic_update_slice_in_dim(wide, shared, kv_at, axis=3)
    wide = lax.psum(wide, "tensor").astype(f32)
    all_gains = lax.psum(jnp.stack(gain_grads), ("dp", "ctx", "tensor"))
    share = norm_gains.shape[1]
    grad_gains = lax.dynamic_slice_in_dim(
        all_gains, (2 * plan.z + plan.x) * share, share, axis=1
    )
    return (
        output[:, None],
        grad_input[:, None],
        stack(lambda r: r[0][:, :qw]).astype(f32),
        wide[:, 0],
        wide[:, 1],
        stack(lambda r: r[0][:, qw + 2 * kw :].T).astype(f32),
        stack(lambda r: r[1]).astype(f32),
        stack(lambda r: r[2]).astype(f32),
        stack(lambda r: r[3].T).astype(f32),
        grad_gains,
    )


def solution(mesh):
    placed = (
        P(None, "dp", "ctx", None),
        P(None, "dp", None),
        P(None, ("dp", "ctx"), "tensor"),
        P(None, ("dp", "ctx"), None),
        P(None, ("dp", "ctx"), None),
        P(None, "tensor", ("dp", "ctx")),
        P(None, ("dp", "ctx"), "tensor"),
        P(None, ("dp", "ctx"), "tensor"),
        P(None, "tensor", ("dp", "ctx")),
        P(None, ("dp", "ctx")),
        P(None, "dp", "ctx", None),
    )
    return jax.shard_map(
        local,
        mesh=mesh,
        in_specs=placed,
        out_specs=(
            P(None, "dp", "ctx", None),
            P(None, "dp", "ctx", None),
            P(None, ("dp", "ctx"), "tensor"),
            P(None, ("dp", "ctx"), None),
            P(None, ("dp", "ctx"), None),
            P(None, "tensor", ("dp", "ctx")),
            P(None, ("dp", "ctx"), "tensor"),
            P(None, ("dp", "ctx"), "tensor"),
            P(None, "tensor", ("dp", "ctx")),
            P(None, ("dp", "ctx")),
        ),
        check_vma=False,
    )
```

```python
import jax
import jax.numpy as jnp
from jax import lax
from jax.sharding import PartitionSpec as P

HQ = 20
HK = 5
HD = 64
LAYERS = 2
GROUP_SIZE = HQ // HK

epsilon = 1e-05
rope_base = 10000.0

f32 = jnp.float32
bf16 = jnp.bfloat16


def product(left_side, right_side, contract):
    return lax.dot_general(
        left_side, right_side, (contract, ((), ())), preferred_element_type=f32
    )


def rotate(values, cosine, sine_value):
    half_size = values.shape[-1] // 2
    first_half = values[..., :half_size]
    second_half = values[..., half_size:]
    return jnp.concatenate(
        [
            first_half * cosine - second_half * sine_value,
            second_half * cosine + first_half * sine_value,
        ],
        axis=-1,
    )


def scale_of(values):
    return lax.rsqrt(jnp.mean(values * values, axis=-1, keepdims=True) + epsilon)


def norm_back(gradient, values, scaling, gain_vector):
    scaled = gradient * gain_vector
    cubed = scaling * scaling * scaling
    return scaling * scaled - values * cubed * jnp.mean(scaled * values, axis=-1, keepdims=True)


class Plan:
    def __init__(self):
        self.n = lax.axis_size("dp")
        self.nt = lax.axis_size("tensor")
        assert lax.axis_size("ctx") == 2 and self.nt == 4
        self.z = lax.axis_index("dp")
        self.x = lax.axis_index("ctx")
        self.t = lax.axis_index("tensor")
        self.y = self.t // 2
        self.c = self.t % 2
        nt = self.nt
        places = [(a, b, d) for a in range(2) for b in range(2) for d in range(2)]
        self.peers = {}
        for j in range(1, 4):
            self.peers[j] = [
                (a * nt + 2 * b + d, (a ^ (j // 2)) * nt + 2 * (b ^ (j % 2)) + d)
                for a, b, d in places
            ]
        self.swap_pairs = [(a * nt + 2 * b + d, d * nt + 2 * b + a) for a, b, d in places]
        assert self.n & (self.n - 1) == 0
        self.core_all = [(i, i ^ 1) for i in range(2 * nt)]
        self.core_pairs = [(i, i ^ 1) for i in range(nt)]
        self.up = [(i, (i + 1) % self.n) for i in range(self.n)]
        self.down = [(i, (i - 1) % self.n) for i in range(self.n)]

    def peer(self, value, j):
        return lax.ppermute(value, ("ctx", "tensor"), self.peers[j])

    def swap(self, value):
        return lax.ppermute(value, ("ctx", "tensor"), self.swap_pairs)

    def core(self, value):
        return lax.ppermute(value, "tensor", self.core_pairs)

    def total(self, value):
        for pairs in self.peers[1], self.peers[2], self.core_all:
            value = value + lax.ppermute(value, ("ctx", "tensor"), pairs)
        step = 1
        while step < self.n:
            value = value + lax.ppermute(value, "dp", [(i, i ^ step) for i in range(self.n)])
            step *= 2
        return value

    def weight_term(self, left, right):
        half = left.shape[1] // 2
        away = self.core(product(left[:, half:], right, ((0,), (0,))).astype(bf16))
        return (product(left[:, :half], right, ((0,), (0,))) + away.astype(f32)).astype(bf16)

    def scatter(self, term):
        return lax.psum_scatter(term, "dp", scatter_dimension=0, tiled=True)

    def into(self, rows, halves):
        half = rows.shape[1] // 2
        return product(rows[:, :half], halves[0], ((1,), (0,))) + product(
            rows[:, half:], halves[1], ((1,), (0,))
        )

    def out_of(self, rows, halves):
        return jnp.concatenate(
            [product(rows, part, ((1,), (1,))).astype(bf16) for part in halves], axis=1
        )

    def spread(self, rows):
        return jnp.concatenate([rows] + [self.peer(rows, j) for j in range(1, 4)], axis=0)

    def gather_sum(self, terms, beside=()):
        rows = terms.shape[0] // 4
        moved = [self.peer(terms[j * rows : (j + 1) * rows], j) for j in range(1, 4)]
        moved, beside = lax.optimization_barrier((moved, beside))
        total = terms[:rows].astype(f32)
        for piece in moved:
            total = total + piece.astype(f32)
        return total, beside

    def inward(self, array):
        lead = array.shape[:-1]
        d = array.shape[-1]
        w = d // (2 * self.n)
        parts = array.reshape(lead + (self.n, 2, w))
        even = parts[..., 0, :].reshape(lead + (d // 2,))
        odd = parts[..., 1, :].reshape(lead + (d // 2,))
        return jnp.where(
            self.c == 0,
            jnp.concatenate([even, odd], axis=-1),
            jnp.concatenate([odd, even], axis=-1),
        )

    def outward(self, array):
        lead = array.shape[:-1]
        d = array.shape[-1]
        w = d // (2 * self.n)
        own = array[..., : d // 2].reshape(lead + (self.n, w))
        other = array[..., d // 2 :].reshape(lead + (self.n, w))
        return jnp.where(
            self.c == 0,
            jnp.stack([own, other], axis=-2),
            jnp.stack([other, own], axis=-2),
        ).reshape(lead + (d,))

    def replicate(self, rows):
        beside = self.peer(rows, 1)
        half = jnp.where(
            self.y == 0,
            jnp.concatenate([rows, beside], axis=0),
            jnp.concatenate([beside, rows], axis=0),
        )
        other = self.core(half)
        return jnp.where(self.c == 0, jnp.stack([half, other]), jnp.stack([other, half]))


def pairs_of(rows, first_pair):
    return jnp.where(first_pair[:, None, None], rows[None, :, 0], rows[None, :, 1])


def attend(queries, key_heads, value_heads, allowed):
    scores = (
        jnp.einsum("hqd,hkd->hqk", queries, key_heads, preferred_element_type=f32) * HD ** (-0.5)
    )
    masked = jnp.where(allowed, scores, -1e30)
    highest = jnp.max(masked, axis=-1, keepdims=True)
    exponent = jnp.where(allowed, jnp.exp(masked - highest), 0.0)
    row_total = jnp.sum(exponent, axis=-1, keepdims=True)
    live_rows = row_total > 0.0
    safe_total = jnp.where(live_rows, row_total, 1.0)
    probability = (exponent / safe_total).astype(bf16)
    mixed = jnp.einsum("hqk,hkd->hqd", probability, value_heads, preferred_element_type=f32)
    merged = jnp.where(live_rows, highest + jnp.log(safe_total), 0.0)
    return mixed, merged


def attend_back(queries, key_heads, value_heads, grad_mixed, merged, allowed):
    scores = (
        jnp.einsum("hqd,hkd->hqk", queries, key_heads, preferred_element_type=f32) * HD ** (-0.5)
    )
    probability = jnp.where(allowed, jnp.exp(scores - merged), 0.0)
    grad_value_heads = jnp.einsum(
        "hqk,hqd->hkd", probability.astype(bf16), grad_mixed, preferred_element_type=f32
    )
    grad_prob = jnp.einsum("hqd,hkd->hqk", grad_mixed, value_heads, preferred_element_type=f32)
    row_delta = jnp.sum(probability * grad_prob, axis=-1, keepdims=True)
    grad_scores = (probability * (grad_prob - row_delta)).astype(bf16)
    grad_queries = jnp.einsum(
        "hqk,hkd->hqd", grad_scores, key_heads, preferred_element_type=f32
    ) * HD ** (-0.5)
    grad_key_heads = jnp.einsum(
        "hqk,hqd->hkd", grad_scores, queries, preferred_element_type=f32
    ) * HD ** (-0.5)
    return grad_queries, grad_key_heads, grad_value_heads


def local(
    tokens, doc_lengths, w_query, w_key, w_value, w_out, w_gate, w_up, w_down, norm_gains, cotangent
):
    plan = Plan()
    micro_count, sequences, half_rows, width = tokens.shape
    assert micro_count == 2 and sequences == 1
    quarter = half_rows // 2
    heads = w_query.shape[2] // HD
    n = plan.n
    group = 2 * plan.y + plan.x
    qw, kw = heads * HD, 2 * HD

    kv_at = plan.t * heads // GROUP_SIZE * HD
    hidden_units = w_gate.shape[2]
    shards = []
    for layer in range(LAYERS):
        keys = lax.dynamic_slice_in_dim(w_key[layer], kv_at, kw, axis=1)
        values = lax.dynamic_slice_in_dim(w_value[layer], kv_at, kw, axis=1)
        shards.append(jnp.concatenate([w_query[layer], keys, values, w_out[layer].T], axis=1))
        ffn_parts = [w_gate[layer], w_up[layer], w_down[layer].T]
        if layer + 1 < LAYERS:
            shards.append(jnp.concatenate(ffn_parts, axis=1))
        else:
            shards.append(jnp.concatenate(ffn_parts[:2], axis=1))
            shards.append(ffn_parts[2])
    swapped = []
    for shard in shards:
        if swapped:
            shard, swapped[-1] = lax.optimization_barrier((shard, swapped[-1]))
        swapped.append(plan.swap(shard))
    owned = []
    for shard in swapped:
        if owned:
            shard, owned[-1] = lax.optimization_barrier((shard, owned[-1]))
        owned.append(lax.all_gather(shard, "dp", axis=0, tiled=True))

    def columns(halves, start, stop):
        return tuple(part[:, start:stop] for part in halves)

    def both_parities(own, after=None):
        if after is not None:
            own, after = lax.optimization_barrier((own, after))
        return (own, plan.core(own)), after

    side = lax.ppermute(norm_gains, "ctx", [(0, 1), (1, 0)])
    pair = jnp.where(
        plan.x == 0,
        jnp.concatenate([norm_gains, side], axis=1),
        jnp.concatenate([side, norm_gains], axis=1),
    )
    gain_pieces = [pair]
    for _ in range(1, n):
        gain_pieces.append(lax.ppermute(gain_pieces[-1], "dp", plan.down))
    ring = jnp.concatenate(gain_pieces + gain_pieces, axis=1)
    gain_width = pair.shape[1]
    gains = lax.dynamic_slice_in_dim(
        ring, (n - plan.z) % n * gain_width, n * gain_width, axis=1
    ).astype(f32)
    gain_attn = plan.inward(gains[:, :width])
    gain_ffn = plan.inward(gains[:, width : 2 * width])
    gain_query = gains[:, 2 * width : 2 * width + HD]
    gain_key = gains[:, 2 * width + HD :]

    blocks = jnp.arange(4, dtype=jnp.int32) ^ (2 * plan.x + plan.y).astype(jnp.int32)
    places = (blocks[:, None] * quarter + jnp.arange(quarter, dtype=jnp.int32)[None, :]).reshape(-1)
    lengths = lax.dynamic_index_in_dim(doc_lengths, plan.c, axis=0, keepdims=False)[0]
    docs = lengths.shape[0]
    ends = jnp.cumsum(lengths, dtype=jnp.int32)
    starts = ends - lengths
    document = jnp.sum((places[:, None] >= ends[None, :]).astype(jnp.int32), axis=-1)
    chosen = document[:, None] == jnp.arange(docs, dtype=jnp.int32)[None, :]
    position = places - jnp.sum(jnp.where(chosen, starts[None, :], 0), axis=-1)
    segment = jnp.where(document < docs, document, -1)
    allowed = (
        (segment[:, None] == segment[None, :])
        & (segment[:, None] >= 0)
        & (places[None, :] <= places[:, None])
    )[None]
    frequency = rope_base ** (-jnp.arange(HD // 2, dtype=f32) * (2.0 / HD))
    angle = position.astype(f32)[:, None] * frequency
    cosine, sine_value = jnp.cos(angle), jnp.sin(angle)
    pair_start = group * heads // GROUP_SIZE
    first_pair = (
        group * heads + jnp.arange(heads, dtype=jnp.int32)
    ) // GROUP_SIZE == pair_start
    weight_first = first_pair.astype(f32)[:, None, None]

    def own_half(array):
        rows = lax.dynamic_index_in_dim(array, plan.c, axis=0, keepdims=False)[0]
        rows = jnp.where(plan.y == 0, rows, jnp.roll(rows, quarter, axis=0))
        return plan.inward(rows)

    def by_head(array, count):
        return jnp.swapaxes(array.reshape(array.shape[0], count, HD), 0, 1)

    def flat(array):
        return jnp.swapaxes(array, 0, 1).reshape(array.shape[1], -1)

    first_half = own_half(tokens)
    cot_half = own_half(cotangent)
    cot_all = jnp.concatenate([cot_half, plan.peer(cot_half, 2)], axis=0)
    tokens_all = jnp.concatenate([first_half, plan.peer(first_half, 2)], axis=0).astype(f32)
    start_grad = jnp.where(segment[:, None] >= 0, cot_all, jnp.zeros_like(cot_all))

    state = tokens_all[:quarter]
    stored = []
    fetched = []
    attn_w, _ = both_parities(owned[0])
    for layer in range(LAYERS):
        w_qkv = columns(attn_w, 0, qw + 2 * kw)
        w_o = columns(attn_w, qw + 2 * kw, None)
        if layer == 0:
            scale_in = scale_of(tokens_all)
            normed = (tokens_all * scale_in * gain_attn[layer]).astype(bf16)
            scale_in = scale_in[:quarter]
        else:
            scale_in = scale_of(state)
            normed = plan.spread((state * scale_in * gain_attn[layer]).astype(bf16))
        qkv = plan.into(normed, w_qkv)
        queries = by_head(qkv[:, :qw], heads)
        query_scale = scale_of(queries)
        query_low = rotate(queries * query_scale * gain_query[layer], cosine, sine_value).astype(
            bf16
        )
        keys = by_head(qkv[:, qw : qw + kw], 2)
        key_scale = scale_of(keys)
        key_low = rotate(keys * key_scale * gain_key[layer], cosine, sine_value).astype(bf16)
        value_low = by_head(qkv[:, qw + kw :].astype(bf16), 2)
        key_heads = jnp.where(first_pair[:, None, None], key_low[0][None], key_low[1][None])
        value_heads = jnp.where(first_pair[:, None, None], value_low[0][None], value_low[1][None])
        mixed, merged = attend(query_low, key_heads, value_heads, allowed)
        mixed_low = flat(mixed.astype(bf16))
        attn_terms = plan.out_of(mixed_low, w_o)
        attn, _ = plan.gather_sum(attn_terms)
        middle = state + attn
        ffn_w, later_middle = both_parities(owned[2 * layer + 1], middle)
        w_g = columns(ffn_w, 0, hidden_units)
        w_u = columns(ffn_w, hidden_units, 2 * hidden_units)
        w_gu = columns(ffn_w, 0, 2 * hidden_units)
        scale_mid = scale_of(middle)
        normed2 = plan.spread((middle * scale_mid * gain_ffn[layer]).astype(bf16))
        gate = plan.into(normed2, w_g)
        up = plan.into(normed2, w_u)
        hidden = (jax.nn.silu(gate) * up).astype(bf16)
        if layer + 1 < LAYERS:
            w_d = columns(ffn_w, 2 * hidden_units, None)
            ffn_terms = plan.out_of(hidden, w_d)
            attn_next, hidden = both_parities(owned[2 * layer + 2], hidden)
        else:
            w_d, normed2 = both_parities(owned[-1], normed2)
            ffn_terms = plan.out_of(hidden, w_d)
        fetched.append((w_qkv, w_o, w_d, w_gu))
        ffn, _ = plan.gather_sum(ffn_terms)
        stored.append(
            (
                state,
                scale_in,
                normed,
                queries,
                query_scale,
                query_low,
                keys,
                key_scale,
                key_heads,
                value_heads,
                merged,
                mixed_low,
                middle,
                scale_mid,
                normed2,
                gate,
                up,
                hidden,
            )
        )
        state = later_middle + ffn
        attn_w = attn_next
    output = plan.replicate(plan.outward(state.astype(bf16)))

    gradient = start_grad[:quarter].astype(f32)
    grad_ffn = start_grad
    results = [[None] * 3 for _ in range(LAYERS)]
    last = []

    def scatter_next(layer, member, term):
        if last:
            at, part = last[-1]
            term, results[at][part] = lax.optimization_barrier((term, results[at][part]))
        results[layer][member] = plan.scatter(term)
        last.append((layer, member))

    gain_grads = [None] * LAYERS
    for layer in reversed(range(LAYERS)):
        w_qkv, w_o, w_d, w_gu = fetched[layer]
        (
            state,
            scale_in,
            normed,
            queries,
            query_scale,
            query_low,
            keys,
            key_scale,
            key_heads,
            value_heads,
            merged,
            mixed_low,
            middle,
            scale_mid,
            normed2,
            gate,
            up,
            hidden,
        ) = stored[layer]
        if grad_ffn is None:
            grad_ffn = plan.spread(gradient.astype(bf16))
        term_d = plan.weight_term(grad_ffn, hidden)
        if layer + 1 == LAYERS:
            w_d, term_d = lax.optimization_barrier((w_d, term_d))
        grad_hidden = plan.into(grad_ffn, w_d)
        sigmoid_gate = jax.nn.sigmoid(gate)
        grad_gate = (
            grad_hidden * up * sigmoid_gate * (1.0 + gate * (1.0 - sigmoid_gate))
        ).astype(bf16)
        grad_up = (grad_hidden * (gate * sigmoid_gate)).astype(bf16)
        grad_gu = jnp.concatenate([grad_gate, grad_up], axis=1)
        term_gu = plan.weight_term(normed2, grad_gu)
        if layer + 1 == LAYERS:
            scatter_next(layer, 2, term_d)
            summed_mid, term_gu = plan.gather_sum(plan.out_of(grad_gu, w_gu), term_gu)
        else:
            summed_mid, (term_d, term_gu) = plan.gather_sum(
                plan.out_of(grad_gu, w_gu), (term_d, term_gu)
            )
            scatter_next(layer, 2, term_d)
        scatter_next(layer, 1, term_gu)
        grad_g_ffn = jnp.sum(summed_mid * middle * scale_mid, axis=0)
        grad_mid = gradient + norm_back(summed_mid, middle, scale_mid, gain_ffn[layer])
        grad_attn = plan.spread(grad_mid.astype(bf16))
        grad_mixed = by_head(plan.into(grad_attn, w_o).astype(bf16), heads)
        term_o = plan.weight_term(grad_attn, mixed_low)
        grad_query_rot, grad_key_heads, grad_value_heads = attend_back(
            query_low, key_heads, value_heads, grad_mixed, merged, allowed
        )
        grad_key_rot = jnp.stack(
            [
                jnp.sum(grad_key_heads * weight_first, axis=0),
                jnp.sum(grad_key_heads * (1.0 - weight_first), axis=0),
            ]
        )
        grad_values = jnp.concatenate(
            [
                jnp.sum(grad_value_heads * weight_first, axis=0),
                jnp.sum(grad_value_heads * (1.0 - weight_first), axis=0),
            ],
            axis=1,
        ).astype(bf16)
        grad_query_norm = rotate(grad_query_rot, cosine, -sine_value)
        grad_g_query = jnp.sum(grad_query_norm * queries * query_scale, axis=(0, 1))
        grad_queries = flat(
            norm_back(grad_query_norm, queries, query_scale, gain_query[layer]).astype(bf16)
        )
        grad_key_norm = rotate(grad_key_rot, cosine, -sine_value)
        grad_g_key = jnp.sum(grad_key_norm * keys * key_scale, axis=(0, 1))
        grad_keys = flat(norm_back(grad_key_norm, keys, key_scale, gain_key[layer]).astype(bf16))
        grad_qkv = jnp.concatenate([grad_queries, grad_keys, grad_values], axis=1)
        term_qkv = plan.weight_term(normed, grad_qkv)
        summed_in, (term_o, term_qkv) = plan.gather_sum(
            plan.out_of(grad_qkv, w_qkv), (term_o, term_qkv)
        )
        scatter_next(layer, 0, jnp.concatenate([term_qkv, term_o], axis=1))
        grad_g_attn = jnp.sum(summed_in * state * scale_in, axis=0)
        gradient = grad_mid + norm_back(summed_in, state, scale_in, gain_attn[layer])
        grad_ffn = None
        gain_grads[layer] = jnp.concatenate(
            [plan.outward(grad_g_attn), plan.outward(grad_g_ffn), grad_g_query, grad_g_key]
        )
    grad_input = plan.replicate(plan.outward(gradient.astype(bf16))).astype(f32)

    for layer in range(LAYERS):
        results[layer] = [plan.swap(term) for term in results[layer]]

    def stack(pick):
        return jnp.stack([pick(results[layer]) for layer in range(LAYERS)])

    shared = stack(lambda r: r[0][:, qw : qw + 2 * kw])
    wide_keys = jnp.zeros(shared.shape[:-1] + (w_key.shape[2],), f32)
    wide_values = wide_keys
    for j in range(plan.nt):
        part = shared
        if j:
            part = lax.ppermute(shared, "tensor", [(i, i ^ j) for i in range(plan.nt)])
        part = part.astype(f32)
        at = (plan.t ^ j) * heads // GROUP_SIZE * HD
        zeros = jnp.zeros_like(wide_keys)
        wide_keys += lax.dynamic_update_slice_in_dim(zeros, part[..., :kw], at, axis=2)
        wide_values += lax.dynamic_update_slice_in_dim(zeros, part[..., kw:], at, axis=2)
    all_gains = plan.total(jnp.stack(gain_grads))
    share = norm_gains.shape[1]
    grad_gains = lax.dynamic_slice_in_dim(
        all_gains, (2 * plan.z + plan.x) * share, share, axis=1
    )
    return (
        output[:, None],
        grad_input[:, None],
        stack(lambda r: r[0][:, :qw]).astype(f32),
        wide_keys,
        wide_values,
        stack(lambda r: r[0][:, qw + 2 * kw :].T).astype(f32),
        stack(lambda r: r[1][:, :hidden_units]).astype(f32),
        stack(lambda r: r[1][:, hidden_units:]).astype(f32),
        stack(lambda r: r[2].T).astype(f32),
        grad_gains,
    )


def solution(mesh):
    placed = (
        P(None, "dp", "ctx", None),
        P(None, "dp", None),
        P(None, ("dp", "ctx"), "tensor"),
        P(None, ("dp", "ctx"), None),
        P(None, ("dp", "ctx"), None),
        P(None, "tensor", ("dp", "ctx")),
        P(None, ("dp", "ctx"), "tensor"),
        P(None, ("dp", "ctx"), "tensor"),
        P(None, "tensor", ("dp", "ctx")),
        P(None, ("dp", "ctx")),
        P(None, "dp", "ctx", None),
    )
    return jax.shard_map(
        local,
        mesh=mesh,
        in_specs=placed,
        out_specs=(
            P(None, "dp", "ctx", None),
            P(None, "dp", "ctx", None),
            P(None, ("dp", "ctx"), "tensor"),
            P(None, ("dp", "ctx"), None),
            P(None, ("dp", "ctx"), None),
            P(None, "tensor", ("dp", "ctx")),
            P(None, ("dp", "ctx"), "tensor"),
            P(None, ("dp", "ctx"), "tensor"),
            P(None, "tensor", ("dp", "ctx")),
            P(None, ("dp", "ctx")),
        ),
        check_vma=False,
    )
```

```python
import jax
import jax.numpy as jnp
from jax import lax
from jax.experimental import pallas as pl
from jax.experimental.pallas import tpu as pltpu
from jax.sharding import PartitionSpec as P

HQ = 20
HK = 5
HD = 64
LAYERS = 2
GROUP_SIZE = HQ // HK

epsilon = 1e-05
rope_base = 10000.0

f32 = jnp.float32
bf16 = jnp.bfloat16


def product(left_side, right_side, contract):
    return lax.dot_general(
        left_side, right_side, (contract, ((), ())), preferred_element_type=f32
    )


def rotate(values, cosine, sine_value):
    half_size = values.shape[-1] // 2
    first_half = values[..., :half_size]
    second_half = values[..., half_size:]
    return jnp.concatenate(
        [
            first_half * cosine - second_half * sine_value,
            second_half * cosine + first_half * sine_value,
        ],
        axis=-1,
    )


def scale_of(values):
    return lax.rsqrt(jnp.mean(values * values, axis=-1, keepdims=True) + epsilon)


def norm_back(gradient, values, scaling, gain_vector):
    scaled = gradient * gain_vector
    cubed = scaling * scaling * scaling
    return scaling * scaled - values * cubed * jnp.mean(scaled * values, axis=-1, keepdims=True)


PARTS = 2


def join_kernel(terms, state, gain, middle, normed, inbox, sum_send, sum_recv, row_send, row_recv):
    x, t = lax.axis_index("ctx"), lax.axis_index("tensor")
    other_x, other_t = 1 - x, t + 2 - 4 * (t // 2)
    peers = [
        {"ctx": x, "tensor": other_t},
        {"ctx": other_x, "tensor": t},
        {"ctx": other_x, "tensor": other_t},
    ]
    rows = state.shape[0]
    step = rows // PARTS
    barrier = pltpu.get_barrier_semaphore()
    for peer in peers:
        pl.semaphore_signal(barrier, inc=1, device_id=peer, device_id_type=pl.DeviceIdType.MESH)
    pl.semaphore_wait(barrier, len(peers))

    def sum_copy(part, j):
        return pltpu.make_async_remote_copy(
            src_ref=terms.at[pl.ds((j + 1) * rows + part * step, step)],
            dst_ref=inbox.at[part, j],
            send_sem=sum_send.at[part, j],
            recv_sem=sum_recv.at[part, j],
            device_id=peers[j],
            device_id_type=pl.DeviceIdType.MESH,
        )

    def row_copy(part, j):
        return pltpu.make_async_remote_copy(
            src_ref=normed.at[pl.ds(part * step, step)],
            dst_ref=normed.at[pl.ds((j + 1) * rows + part * step, step)],
            send_sem=row_send.at[part, j],
            recv_sem=row_recv.at[part, j],
            device_id=peers[j],
            device_id_type=pl.DeviceIdType.MESH,
        )

    for part in range(PARTS):
        for j in (2, 1, 0):
            sum_copy(part, j).start()
    for part in range(PARTS):
        here = pl.ds(part * step, step)
        total = terms[here].astype(f32)
        for j in range(3):
            sum_copy(part, j).wait_recv()
            total = total + inbox[part, j].astype(f32)
        total = state[here] + total
        middle[here] = total
        normed[here] = (total * scale_of(total) * gain[...]).astype(bf16)
        for j in (2, 1, 0):
            row_copy(part, j).start()
    for part in range(PARTS):
        for j in range(3):
            sum_copy(part, j).wait_send()
            row_copy(part, j).wait_send()
            row_copy(part, j).wait_recv()


def join(terms, state, gain):
    rows, width = state.shape
    whole = pl.BlockSpec(memory_space=pltpu.VMEM)
    return pl.pallas_call(
        join_kernel,
        out_shape=(
            jax.ShapeDtypeStruct((rows, width), f32),
            jax.ShapeDtypeStruct((4 * rows, width), bf16),
        ),
        in_specs=[whole] * 3,
        out_specs=(whole, whole),
        scratch_shapes=[pltpu.VMEM((PARTS, 3, rows // PARTS, width), bf16)]
        + [pltpu.SemaphoreType.DMA((PARTS, 3))] * 4,
        compiler_params=pltpu.CompilerParams(
            collective_id=0, has_side_effects=True, vmem_limit_bytes=32 * 2**20
        ),
        cost_estimate=pl.CostEstimate(flops=1000, bytes_accessed=1000, transcendentals=0),
        name="join",
    )(terms, state, gain[None])


class Plan:
    def __init__(self):
        self.n = lax.axis_size("dp")
        self.nt = lax.axis_size("tensor")
        assert lax.axis_size("ctx") == 2 and self.nt == 4
        self.z = lax.axis_index("dp")
        self.x = lax.axis_index("ctx")
        self.t = lax.axis_index("tensor")
        self.y = self.t // 2
        self.c = self.t % 2
        nt = self.nt
        places = [(a, b, d) for a in range(2) for b in range(2) for d in range(2)]
        self.peers = {}
        for j in range(1, 4):
            self.peers[j] = [
                (a * nt + 2 * b + d, (a ^ (j // 2)) * nt + 2 * (b ^ (j % 2)) + d)
                for a, b, d in places
            ]
        self.swap_pairs = [
            (a * nt + 2 * b + d, d * nt + 2 * b + a) for a, b, d in places if a != d
        ]
        self.cross_pairs = {
            j: [
                (a * nt + 2 * b + d, d * nt + 2 * (b ^ (j // 2)) + (a ^ (j % 2)))
                for a, b, d in places
            ]
            for j in range(1, 4)
        }
        assert self.n & (self.n - 1) == 0
        self.core_all = [(i, i ^ 1) for i in range(2 * nt)]
        self.core_pairs = [(i, i ^ 1) for i in range(nt)]
        self.up = [(i, (i + 1) % self.n) for i in range(self.n)]
        self.down = [(i, (i - 1) % self.n) for i in range(self.n)]

    def peer(self, value, j):
        return lax.ppermute(value, ("ctx", "tensor"), self.peers[j])

    def swap(self, value):
        moved = lax.ppermute(value, ("ctx", "tensor"), self.swap_pairs)
        return jnp.where(self.x == self.c, value, moved)

    def cross(self, value, j):
        return lax.ppermute(value, ("ctx", "tensor"), self.cross_pairs[j])

    def core(self, value):
        return lax.ppermute(value, "tensor", self.core_pairs)

    def total(self, value):
        for pairs in self.peers[1], self.peers[2], self.core_all:
            value = value + lax.ppermute(value, ("ctx", "tensor"), pairs)
        step = 1
        while step < self.n:
            value = value + lax.ppermute(value, "dp", [(i, i ^ step) for i in range(self.n)])
            step *= 2
        return value

    def weight_term(self, left, right):
        half = left.shape[1] // 2
        away = self.core(product(left[:, half:], right, ((0,), (0,))).astype(bf16))
        return (product(left[:, :half], right, ((0,), (0,))) + away.astype(f32)).astype(bf16)

    def scatter(self, term):
        return lax.psum_scatter(term, "dp", scatter_dimension=0, tiled=True)

    def into(self, rows, halves):
        half = rows.shape[1] // 2
        return product(rows[:, :half], halves[0], ((1,), (0,))) + product(
            rows[:, half:], halves[1], ((1,), (0,))
        )

    def out_of(self, rows, halves):
        return jnp.concatenate(
            [product(rows, part, ((1,), (1,))).astype(bf16) for part in halves], axis=1
        )

    def spread(self, rows):
        return jnp.concatenate([rows] + [self.peer(rows, j) for j in range(1, 4)], axis=0)

    def spread_beside(self, rows, beside):
        moved = [self.peer(rows, j) for j in range(1, 4)]
        moved, beside = lax.optimization_barrier((moved, beside))
        return jnp.concatenate([rows] + moved, axis=0), beside

    def gather_sum(self, terms, beside=()):
        rows = terms.shape[0] // 4
        moved = [self.peer(terms[j * rows : (j + 1) * rows], j) for j in range(1, 4)]
        moved, beside = lax.optimization_barrier((moved, beside))
        total = terms[:rows].astype(f32)
        for piece in moved:
            total = total + piece.astype(f32)
        return total, beside

    def inward(self, array):
        lead = array.shape[:-1]
        d = array.shape[-1]
        w = d // (2 * self.n)
        parts = array.reshape(lead + (self.n, 2, w))
        even = parts[..., 0, :].reshape(lead + (d // 2,))
        odd = parts[..., 1, :].reshape(lead + (d // 2,))
        return jnp.where(
            self.c == 0,
            jnp.concatenate([even, odd], axis=-1),
            jnp.concatenate([odd, even], axis=-1),
        )

    def outward(self, array):
        lead = array.shape[:-1]
        d = array.shape[-1]
        w = d // (2 * self.n)
        own = array[..., : d // 2].reshape(lead + (self.n, w))
        other = array[..., d // 2 :].reshape(lead + (self.n, w))
        return jnp.where(
            self.c == 0,
            jnp.stack([own, other], axis=-2),
            jnp.stack([other, own], axis=-2),
        ).reshape(lead + (d,))

    def both_quarters(self, rows):
        beside = self.peer(rows, 1)
        return jnp.where(
            self.y == 0,
            jnp.concatenate([rows, beside], axis=0),
            jnp.concatenate([beside, rows], axis=0),
        )

    def both_micro(self, half, other):
        return jnp.where(self.c == 0, jnp.stack([half, other]), jnp.stack([other, half]))


def attend(queries, key_heads, value_heads, allowed):
    scores = (
        jnp.einsum("hqd,hkd->hqk", queries, key_heads, preferred_element_type=f32) * HD ** (-0.5)
    )
    masked = jnp.where(allowed, scores, -1e30)
    highest = jnp.max(masked, axis=-1, keepdims=True)
    exponent = jnp.where(allowed, jnp.exp(masked - highest), 0.0)
    row_total = jnp.sum(exponent, axis=-1, keepdims=True)
    live_rows = row_total > 0.0
    safe_total = jnp.where(live_rows, row_total, 1.0)
    probability = (exponent / safe_total).astype(bf16)
    mixed = jnp.einsum("hqk,hkd->hqd", probability, value_heads, preferred_element_type=f32)
    merged = jnp.where(live_rows, highest + jnp.log(safe_total), 0.0)
    return mixed, merged


def attend_back(queries, key_heads, value_heads, grad_mixed, merged, allowed):
    scores = (
        jnp.einsum("hqd,hkd->hqk", queries, key_heads, preferred_element_type=f32) * HD ** (-0.5)
    )
    probability = jnp.where(allowed, jnp.exp(scores - merged), 0.0)
    grad_value_heads = jnp.einsum(
        "hqk,hqd->hkd", probability.astype(bf16), grad_mixed, preferred_element_type=f32
    )
    grad_prob = jnp.einsum("hqd,hkd->hqk", grad_mixed, value_heads, preferred_element_type=f32)
    row_delta = jnp.sum(probability * grad_prob, axis=-1, keepdims=True)
    grad_scores = (probability * (grad_prob - row_delta)).astype(bf16)
    grad_queries = jnp.einsum(
        "hqk,hkd->hqd", grad_scores, key_heads, preferred_element_type=f32
    ) * HD ** (-0.5)
    grad_key_heads = jnp.einsum(
        "hqk,hqd->hkd", grad_scores, queries, preferred_element_type=f32
    ) * HD ** (-0.5)
    return grad_queries, grad_key_heads, grad_value_heads


def local(
    tokens, doc_lengths, w_query, w_key, w_value, w_out, w_gate, w_up, w_down, norm_gains, cotangent
):
    plan = Plan()
    micro_count, sequences, half_rows, width = tokens.shape
    assert micro_count == 2 and sequences == 1
    quarter = half_rows // 2
    heads = w_query.shape[2] // HD
    n = plan.n
    group = 2 * plan.y + plan.x
    qw, kw = heads * HD, 2 * HD

    kv_at = plan.t * heads // GROUP_SIZE * HD
    hidden_units = w_gate.shape[2]
    attn_width = qw + 2 * kw + qw
    attn_shards = []
    for layer in range(LAYERS):
        keys = lax.dynamic_slice_in_dim(w_key[layer], kv_at, kw, axis=1)
        values = lax.dynamic_slice_in_dim(w_value[layer], kv_at, kw, axis=1)
        attn_shards += [w_query[layer], keys, values, w_out[layer].T]
    swapped = [plan.swap(jnp.concatenate(attn_shards, axis=1))]
    swapped[-1], w_gate, w_up, w_down, tokens, cotangent, norm_gains = lax.optimization_barrier(
        (swapped[-1], w_gate, w_up, w_down, tokens, cotangent, norm_gains)
    )
    for layer in range(LAYERS):
        shard = jnp.concatenate([w_gate[layer], w_up[layer], w_down[layer].T], axis=1)
        if layer:
            shard, swapped[-1] = lax.optimization_barrier((shard, swapped[-1]))
        swapped.append(plan.swap(shard))
    owned = []
    for index, shard in enumerate(swapped):
        if index > 1:
            shard, owned[-1] = lax.optimization_barrier((shard, owned[-1]))
        owned.append(lax.all_gather(shard, "dp", axis=0, tiled=True))

    def columns(halves, start, stop):
        return tuple(part[:, start:stop] for part in halves)

    def both_parities(own, after=None):
        if after is not None:
            own, after = lax.optimization_barrier((own, after))
        return (own, plan.core(own)), after

    side = lax.ppermute(norm_gains, "ctx", [(0, 1), (1, 0)])
    pair = jnp.where(
        plan.x == 0,
        jnp.concatenate([norm_gains, side], axis=1),
        jnp.concatenate([side, norm_gains], axis=1),
    )
    gain_pieces = [pair]
    for _ in range(1, n):
        gain_pieces.append(lax.ppermute(gain_pieces[-1], "dp", plan.down))
    ring = jnp.concatenate(gain_pieces + gain_pieces, axis=1)
    gain_width = pair.shape[1]
    gains = lax.dynamic_slice_in_dim(
        ring, (n - plan.z) % n * gain_width, n * gain_width, axis=1
    ).astype(f32)
    gain_attn = plan.inward(gains[:, :width])
    gain_ffn = plan.inward(gains[:, width : 2 * width])
    gain_query = gains[:, 2 * width : 2 * width + HD]
    gain_key = gains[:, 2 * width + HD :]

    blocks = jnp.arange(4, dtype=jnp.int32) ^ (2 * plan.x + plan.y).astype(jnp.int32)
    places = (blocks[:, None] * quarter + jnp.arange(quarter, dtype=jnp.int32)[None, :]).reshape(-1)
    lengths = lax.dynamic_index_in_dim(doc_lengths, plan.c, axis=0, keepdims=False)[0]
    docs = lengths.shape[0]
    ends = jnp.cumsum(lengths, dtype=jnp.int32)
    starts = ends - lengths
    document = jnp.sum((places[:, None] >= ends[None, :]).astype(jnp.int32), axis=-1)
    chosen = document[:, None] == jnp.arange(docs, dtype=jnp.int32)[None, :]
    position = places - jnp.sum(jnp.where(chosen, starts[None, :], 0), axis=-1)
    segment = jnp.where(document < docs, document, -1)
    allowed = (
        (segment[:, None] == segment[None, :])
        & (segment[:, None] >= 0)
        & (places[None, :] <= places[:, None])
    )[None]
    frequency = rope_base ** (-jnp.arange(HD // 2, dtype=f32) * (2.0 / HD))
    angle = position.astype(f32)[:, None] * frequency
    cosine, sine_value = jnp.cos(angle), jnp.sin(angle)
    pair_start = group * heads // GROUP_SIZE
    first_pair = (
        group * heads + jnp.arange(heads, dtype=jnp.int32)
    ) // GROUP_SIZE == pair_start
    weight_first = first_pair.astype(f32)[:, None, None]

    def own_half(array):
        rows = lax.dynamic_index_in_dim(array, plan.c, axis=0, keepdims=False)[0]
        rows = jnp.where(plan.y == 0, rows, jnp.roll(rows, quarter, axis=0))
        return plan.inward(rows)

    def by_head(array, count):
        return jnp.swapaxes(array.reshape(array.shape[0], count, HD), 0, 1)

    def flat(array):
        return jnp.swapaxes(array, 0, 1).reshape(array.shape[1], -1)

    first_half = own_half(tokens)
    cot_half = own_half(cotangent)
    cot_all = jnp.concatenate([cot_half, plan.peer(cot_half, 2)], axis=0)
    tokens_all = jnp.concatenate([first_half, plan.peer(first_half, 2)], axis=0).astype(f32)
    start_grad = jnp.where(segment[:, None] >= 0, cot_all, jnp.zeros_like(cot_all))

    state = tokens_all[:quarter]
    stored = []
    fetched = []
    attn_all, _ = both_parities(owned[0])
    for layer in range(LAYERS):
        attn_w = columns(attn_all, layer * attn_width, (layer + 1) * attn_width)
        w_qkv = columns(attn_w, 0, qw + 2 * kw)
        w_o = columns(attn_w, qw + 2 * kw, None)
        if layer == 0:
            scale_in = scale_of(tokens_all)
            normed = (tokens_all * scale_in * gain_attn[layer]).astype(bf16)
            normed, start_grad = lax.optimization_barrier((normed, start_grad))
            scale_in = scale_in[:quarter]
        else:
            scale_in = scale_of(state)
            normed = next_normed
        qkv = plan.into(normed, w_qkv)
        queries = by_head(qkv[:, :qw], heads)
        query_scale = scale_of(queries)
        query_low = rotate(queries * query_scale * gain_query[layer], cosine, sine_value).astype(
            bf16
        )
        keys = by_head(qkv[:, qw : qw + kw], 2)
        key_scale = scale_of(keys)
        key_low = rotate(keys * key_scale * gain_key[layer], cosine, sine_value).astype(bf16)
        value_low = by_head(qkv[:, qw + kw :].astype(bf16), 2)
        key_heads = jnp.where(first_pair[:, None, None], key_low[0][None], key_low[1][None])
        value_heads = jnp.where(first_pair[:, None, None], value_low[0][None], value_low[1][None])
        mixed, merged = attend(query_low, key_heads, value_heads, allowed)
        mixed_low = flat(mixed.astype(bf16))
        attn_terms = plan.out_of(mixed_low, w_o)
        middle, normed2 = join(attn_terms, state, gain_ffn[layer])
        ffn_w, later_middle = both_parities(owned[layer + 1], middle)
        w_g = columns(ffn_w, 0, hidden_units)
        w_u = columns(ffn_w, hidden_units, 2 * hidden_units)
        w_gu = columns(ffn_w, 0, 2 * hidden_units)
        scale_mid = scale_of(middle)
        gate = plan.into(normed2, w_g)
        up = plan.into(normed2, w_u)
        hidden = (jax.nn.silu(gate) * up).astype(bf16)
        w_d = columns(ffn_w, 2 * hidden_units, None)
        ffn_terms = plan.out_of(hidden, w_d)
        fetched.append((w_qkv, w_o, w_d, w_gu))
        stored.append(
            (
                state,
                scale_in,
                normed,
                queries,
                query_scale,
                query_low,
                keys,
                key_scale,
                key_heads,
                value_heads,
                merged,
                mixed_low,
                middle,
                scale_mid,
                normed2,
                gate,
                up,
                hidden,
            )
        )
        if layer + 1 < LAYERS:
            state, next_normed = join(ffn_terms, later_middle, gain_attn[layer + 1])

    gradient = start_grad[:quarter].astype(f32)
    grad_ffn = start_grad
    results = [[None] * 3 for _ in range(LAYERS)]
    last = []

    def finish(term):
        moved = plan.swap(term)
        keys = jnp.zeros((term.shape[0], w_key.shape[2]), f32)
        values = keys
        for j in range(plan.nt):
            part = moved[:, qw : qw + 2 * kw] if j == 0 else plan.cross(term[:, qw : qw + 2 * kw], j)
            part = part.astype(f32)
            sender = 2 * (plan.y ^ (j // 2)) + (plan.c ^ (j % 2))
            at = sender * heads // GROUP_SIZE * HD
            zeros = jnp.zeros_like(keys)
            keys += lax.dynamic_update_slice_in_dim(zeros, part[:, :kw], at, axis=1)
            values += lax.dynamic_update_slice_in_dim(zeros, part[:, kw:], at, axis=1)
        query = moved[:, :qw].astype(f32)
        out = moved[:, qw + 2 * kw :].T.astype(f32)
        return query, keys, values, out

    def scatter_next(layer, member, term):
        if last:
            at, part = last[-1]
            term, results[at][part] = lax.optimization_barrier((term, results[at][part]))
        results[layer][member] = plan.scatter(term)
        last.append((layer, member))

    gain_grads = [None] * LAYERS
    for layer in reversed(range(LAYERS)):
        w_qkv, w_o, w_d, w_gu = fetched[layer]
        (
            state,
            scale_in,
            normed,
            queries,
            query_scale,
            query_low,
            keys,
            key_scale,
            key_heads,
            value_heads,
            merged,
            mixed_low,
            middle,
            scale_mid,
            normed2,
            gate,
            up,
            hidden,
        ) = stored[layer]
        if grad_ffn is None:
            grad_ffn, results[layer + 1][1] = plan.spread_beside(
                gradient.astype(bf16), results[layer + 1][1]
            )
        term_d = plan.weight_term(grad_ffn, hidden)
        if layer + 1 == LAYERS:
            scatter_next(layer, 2, term_d)
        grad_hidden = plan.into(grad_ffn, w_d)
        sigmoid_gate = jax.nn.sigmoid(gate)
        grad_gate = (
            grad_hidden * up * sigmoid_gate * (1.0 + gate * (1.0 - sigmoid_gate))
        ).astype(bf16)
        grad_up = (grad_hidden * (gate * sigmoid_gate)).astype(bf16)
        grad_gu = jnp.concatenate([grad_gate, grad_up], axis=1)
        if layer + 1 < LAYERS:
            above = results[layer + 1]
            ffn_high = plan.swap(jnp.concatenate([above[1], above[2]], axis=1))
            grad_gu, ffn_high, above[0], term_d = lax.optimization_barrier(
                (grad_gu, ffn_high, above[0], term_d)
            )
        term_gu = plan.weight_term(normed2, grad_gu)
        mid_terms = plan.out_of(grad_gu, w_gu)
        if layer + 1 == LAYERS:
            summed_mid, term_gu = plan.gather_sum(mid_terms, term_gu)
        else:
            scatter_next(layer, 2, term_d)
            summed_mid, (results[layer][2], term_gu) = plan.gather_sum(
                mid_terms, (results[layer][2], term_gu)
            )
        scatter_next(layer, 1, term_gu)
        grad_g_ffn = jnp.sum(summed_mid * middle * scale_mid, axis=0)
        grad_mid = gradient + norm_back(summed_mid, middle, scale_mid, gain_ffn[layer])
        grad_attn = plan.spread(grad_mid.astype(bf16))
        grad_mixed = by_head(plan.into(grad_attn, w_o).astype(bf16), heads)
        term_o = plan.weight_term(grad_attn, mixed_low)
        grad_query_rot, grad_key_heads, grad_value_heads = attend_back(
            query_low, key_heads, value_heads, grad_mixed, merged, allowed
        )
        grad_key_rot = jnp.stack(
            [
                jnp.sum(grad_key_heads * weight_first, axis=0),
                jnp.sum(grad_key_heads * (1.0 - weight_first), axis=0),
            ]
        )
        grad_values = jnp.concatenate(
            [
                jnp.sum(grad_value_heads * weight_first, axis=0),
                jnp.sum(grad_value_heads * (1.0 - weight_first), axis=0),
            ],
            axis=1,
        ).astype(bf16)
        grad_query_norm = rotate(grad_query_rot, cosine, -sine_value)
        grad_g_query = jnp.sum(grad_query_norm * queries * query_scale, axis=(0, 1))
        grad_queries = flat(
            norm_back(grad_query_norm, queries, query_scale, gain_query[layer]).astype(bf16)
        )
        grad_key_norm = rotate(grad_key_rot, cosine, -sine_value)
        grad_g_key = jnp.sum(grad_key_norm * keys * key_scale, axis=(0, 1))
        grad_keys = flat(norm_back(grad_key_norm, keys, key_scale, gain_key[layer]).astype(bf16))
        grad_qkv = jnp.concatenate([grad_queries, grad_keys, grad_values], axis=1)
        if layer + 1 < LAYERS:
            attn_high = finish(results[layer + 1][0])
            grad_qkv, attn_high = lax.optimization_barrier((grad_qkv, attn_high))
        term_qkv = plan.weight_term(normed, grad_qkv)
        summed_in, (term_o, term_qkv) = plan.gather_sum(
            plan.out_of(grad_qkv, w_qkv), (term_o, term_qkv)
        )
        scatter_next(layer, 0, jnp.concatenate([term_qkv, term_o], axis=1))
        grad_g_attn = jnp.sum(summed_in * state * scale_in, axis=0)
        gradient = grad_mid + norm_back(summed_in, state, scale_in, gain_attn[layer])
        grad_ffn = None
        gain_grads[layer] = jnp.concatenate(
            [plan.outward(grad_g_attn), plan.outward(grad_g_ffn), grad_g_query, grad_g_key]
        )
    ffn_terms, gradient = lax.optimization_barrier((ffn_terms, gradient))
    ffn, _ = plan.gather_sum(ffn_terms)
    output = plan.both_quarters(plan.outward((later_middle + ffn).astype(bf16)))
    output = (output, plan.core(output))
    grad_input = plan.both_quarters(plan.outward(gradient.astype(bf16)))
    grad_input = (grad_input, plan.core(grad_input))
    all_gains = plan.total(jnp.stack(gain_grads))

    ffn_low = plan.swap(jnp.concatenate([results[0][1], results[0][2]], axis=1))
    grad_down = jnp.stack([ffn[:, 2 * hidden_units :].T for ffn in (ffn_low, ffn_high)])
    attn_low, ffn_low, grad_down, output, grad_input, all_gains = lax.optimization_barrier(
        (results[0][0], ffn_low, grad_down.astype(f32), output, grad_input, all_gains)
    )
    grad_gate = jnp.stack([ffn[:, :hidden_units] for ffn in (ffn_low, ffn_high)])
    grad_up = jnp.stack([ffn[:, hidden_units : 2 * hidden_units] for ffn in (ffn_low, ffn_high)])
    output = plan.both_micro(*output)
    grad_input = plan.both_micro(*grad_input).astype(f32)
    grad_query, grad_key, grad_value, grad_out = (
        jnp.stack(pair) for pair in zip(finish(attn_low), attn_high)
    )
    share = norm_gains.shape[1]
    grad_gains = lax.dynamic_slice_in_dim(
        all_gains, (2 * plan.z + plan.x) * share, share, axis=1
    )
    return (
        output[:, None],
        grad_input[:, None],
        grad_query,
        grad_key,
        grad_value,
        grad_out,
        grad_gate.astype(f32),
        grad_up.astype(f32),
        grad_down,
        grad_gains,
    )


def solution(mesh):
    placed = (
        P(None, "dp", "ctx", None),
        P(None, "dp", None),
        P(None, ("dp", "ctx"), "tensor"),
        P(None, ("dp", "ctx"), None),
        P(None, ("dp", "ctx"), None),
        P(None, "tensor", ("dp", "ctx")),
        P(None, ("dp", "ctx"), "tensor"),
        P(None, ("dp", "ctx"), "tensor"),
        P(None, "tensor", ("dp", "ctx")),
        P(None, ("dp", "ctx")),
        P(None, "dp", "ctx", None),
    )
    return jax.shard_map(
        local,
        mesh=mesh,
        in_specs=placed,
        out_specs=(
            P(None, "dp", "ctx", None),
            P(None, "dp", "ctx", None),
            P(None, ("dp", "ctx"), "tensor"),
            P(None, ("dp", "ctx"), None),
            P(None, ("dp", "ctx"), None),
            P(None, "tensor", ("dp", "ctx")),
            P(None, ("dp", "ctx"), "tensor"),
            P(None, ("dp", "ctx"), "tensor"),
            P(None, "tensor", ("dp", "ctx")),
            P(None, ("dp", "ctx")),
        ),
        check_vma=False,
    )
```

```python
import jax
import jax.numpy as jnp
from jax import lax
from jax.experimental import pallas as pl
from jax.experimental.pallas import tpu as pltpu
from jax.sharding import PartitionSpec as P

HQ = 20
HK = 5
HD = 64
LAYERS = 2
GROUP_SIZE = HQ // HK

epsilon = 1e-05
rope_base = 10000.0

f32 = jnp.float32
bf16 = jnp.bfloat16


def product(left_side, right_side, contract):
    return lax.dot_general(
        left_side, right_side, (contract, ((), ())), preferred_element_type=f32
    )


def rotate(values, cosine, sine_value):
    half_size = values.shape[-1] // 2
    first_half = values[..., :half_size]
    second_half = values[..., half_size:]
    return jnp.concatenate(
        [
            first_half * cosine - second_half * sine_value,
            second_half * cosine + first_half * sine_value,
        ],
        axis=-1,
    )


def scale_of(values):
    return lax.rsqrt(jnp.mean(values * values, axis=-1, keepdims=True) + epsilon)


def norm_back(gradient, values, scaling, gain_vector):
    scaled = gradient * gain_vector
    cubed = scaling * scaling * scaling
    return scaling * scaled - values * cubed * jnp.mean(scaled * values, axis=-1, keepdims=True)


PARTS = 2


def join_kernel(terms, state, gain, middle, normed, inbox, sum_send, sum_recv, row_send, row_recv):
    x, t = lax.axis_index("ctx"), lax.axis_index("tensor")
    other_x, other_t = 1 - x, t + 2 - 4 * (t // 2)
    peers = [
        {"ctx": x, "tensor": other_t},
        {"ctx": other_x, "tensor": t},
        {"ctx": other_x, "tensor": other_t},
    ]
    rows = state.shape[0]
    step = rows // PARTS
    barrier = pltpu.get_barrier_semaphore()
    for peer in peers:
        pl.semaphore_signal(barrier, inc=1, device_id=peer, device_id_type=pl.DeviceIdType.MESH)
    pl.semaphore_wait(barrier, len(peers))

    def sum_copy(part, j):
        return pltpu.make_async_remote_copy(
            src_ref=terms.at[pl.ds((j + 1) * rows + part * step, step)],
            dst_ref=inbox.at[part, j],
            send_sem=sum_send.at[part, j],
            recv_sem=sum_recv.at[part, j],
            device_id=peers[j],
            device_id_type=pl.DeviceIdType.MESH,
        )

    def row_copy(part, j):
        return pltpu.make_async_remote_copy(
            src_ref=normed.at[pl.ds(part * step, step)],
            dst_ref=normed.at[pl.ds((j + 1) * rows + part * step, step)],
            send_sem=row_send.at[part, j],
            recv_sem=row_recv.at[part, j],
            device_id=peers[j],
            device_id_type=pl.DeviceIdType.MESH,
        )

    for part in range(PARTS):
        for j in (2, 1, 0):
            sum_copy(part, j).start()
    for part in range(PARTS):
        here = pl.ds(part * step, step)
        total = terms[here].astype(f32)
        for j in range(3):
            sum_copy(part, j).wait_recv()
            total = total + inbox[part, j].astype(f32)
        total = state[here] + total
        middle[here] = total
        normed[here] = (total * scale_of(total) * gain[...]).astype(bf16)
        for j in (2, 1, 0):
            row_copy(part, j).start()
    for part in range(PARTS):
        for j in range(3):
            sum_copy(part, j).wait_send()
            row_copy(part, j).wait_send()
            row_copy(part, j).wait_recv()


def join(terms, state, gain):
    rows, width = state.shape
    whole = pl.BlockSpec(memory_space=pltpu.VMEM)
    return pl.pallas_call(
        join_kernel,
        out_shape=(
            jax.ShapeDtypeStruct((rows, width), f32),
            jax.ShapeDtypeStruct((4 * rows, width), bf16),
        ),
        in_specs=[whole] * 3,
        out_specs=(whole, whole),
        scratch_shapes=[pltpu.VMEM((PARTS, 3, rows // PARTS, width), bf16)]
        + [pltpu.SemaphoreType.DMA((PARTS, 3))] * 4,
        compiler_params=pltpu.CompilerParams(
            collective_id=0, has_side_effects=True, vmem_limit_bytes=32 * 2**20
        ),
        cost_estimate=pl.CostEstimate(flops=1000, bytes_accessed=1000, transcendentals=0),
        name="join",
    )(terms, state, gain[None])


class Plan:
    def __init__(self):
        self.n = lax.axis_size("dp")
        self.nt = lax.axis_size("tensor")
        assert lax.axis_size("ctx") == 2 and self.nt == 4
        self.z = lax.axis_index("dp")
        self.x = lax.axis_index("ctx")
        self.t = lax.axis_index("tensor")
        self.y = self.t // 2
        self.c = self.t % 2
        nt = self.nt
        places = [(a, b, d) for a in range(2) for b in range(2) for d in range(2)]
        self.peers = {}
        for j in range(1, 4):
            self.peers[j] = [
                (a * nt + 2 * b + d, (a ^ (j // 2)) * nt + 2 * (b ^ (j % 2)) + d)
                for a, b, d in places
            ]
        self.swap_pairs = [
            (a * nt + 2 * b + d, d * nt + 2 * b + a) for a, b, d in places if a != d
        ]
        self.cross_pairs = {
            j: [
                (a * nt + 2 * b + d, d * nt + 2 * (b ^ (j // 2)) + (a ^ (j % 2)))
                for a, b, d in places
            ]
            for j in range(1, 4)
        }
        assert self.n & (self.n - 1) == 0
        self.core_all = [(i, i ^ 1) for i in range(2 * nt)]
        self.core_pairs = [(i, i ^ 1) for i in range(nt)]
        self.up = [(i, (i + 1) % self.n) for i in range(self.n)]
        self.down = [(i, (i - 1) % self.n) for i in range(self.n)]

    def peer(self, value, j):
        return lax.ppermute(value, ("ctx", "tensor"), self.peers[j])

    def swap(self, value):
        moved = lax.ppermute(value, ("ctx", "tensor"), self.swap_pairs)
        return jnp.where(self.x == self.c, value, moved)

    def cross(self, value, j):
        return lax.ppermute(value, ("ctx", "tensor"), self.cross_pairs[j])

    def core(self, value):
        return lax.ppermute(value, "tensor", self.core_pairs)

    def total(self, value):
        for pairs in self.peers[1], self.peers[2], self.core_all:
            value = value + lax.ppermute(value, ("ctx", "tensor"), pairs)
        step = 1
        while step < self.n:
            value = value + lax.ppermute(value, "dp", [(i, i ^ step) for i in range(self.n)])
            step *= 2
        return value

    def weight_term(self, left, right):
        half = left.shape[1] // 2
        away = self.core(product(left[:, half:], right, ((0,), (0,))).astype(bf16))
        return (product(left[:, :half], right, ((0,), (0,))) + away.astype(f32)).astype(bf16)

    def scatter(self, term):
        return lax.psum_scatter(term, "dp", scatter_dimension=0, tiled=True)

    def into(self, rows, halves):
        half = rows.shape[1] // 2
        return product(rows[:, :half], halves[0], ((1,), (0,))) + product(
            rows[:, half:], halves[1], ((1,), (0,))
        )

    def out_of(self, rows, halves):
        return jnp.concatenate(
            [product(rows, part, ((1,), (1,))).astype(bf16) for part in halves], axis=1
        )

    def spread(self, rows):
        return jnp.concatenate([rows] + [self.peer(rows, j) for j in range(1, 4)], axis=0)

    def spread_beside(self, rows, beside):
        moved = [self.peer(rows, j) for j in range(1, 4)]
        moved, beside = lax.optimization_barrier((moved, beside))
        return jnp.concatenate([rows] + moved, axis=0), beside

    def gather_sum(self, terms, beside=()):
        rows = terms.shape[0] // 4
        moved = [self.peer(terms[j * rows : (j + 1) * rows], j) for j in range(1, 4)]
        moved, beside = lax.optimization_barrier((moved, beside))
        total = terms[:rows].astype(f32)
        for piece in moved:
            total = total + piece.astype(f32)
        return total, beside

    def inward(self, array):
        lead = array.shape[:-1]
        d = array.shape[-1]
        w = d // (2 * self.n)
        parts = array.reshape(lead + (self.n, 2, w))
        even = parts[..., 0, :].reshape(lead + (d // 2,))
        odd = parts[..., 1, :].reshape(lead + (d // 2,))
        return jnp.where(
            self.c == 0,
            jnp.concatenate([even, odd], axis=-1),
            jnp.concatenate([odd, even], axis=-1),
        )

    def outward(self, array):
        lead = array.shape[:-1]
        d = array.shape[-1]
        w = d // (2 * self.n)
        own = array[..., : d // 2].reshape(lead + (self.n, w))
        other = array[..., d // 2 :].reshape(lead + (self.n, w))
        return jnp.where(
            self.c == 0,
            jnp.stack([own, other], axis=-2),
            jnp.stack([other, own], axis=-2),
        ).reshape(lead + (d,))

    def both_quarters(self, rows):
        beside = self.peer(rows, 1)
        return jnp.where(
            self.y == 0,
            jnp.concatenate([rows, beside], axis=0),
            jnp.concatenate([beside, rows], axis=0),
        )

    def both_micro(self, half, other):
        return jnp.where(self.c == 0, jnp.stack([half, other]), jnp.stack([other, half]))


def attend(queries, key_heads, value_heads, allowed):
    scores = (
        jnp.einsum("hqd,hkd->hqk", queries, key_heads, preferred_element_type=f32) * HD ** (-0.5)
    )
    masked = jnp.where(allowed, scores, -1e30)
    highest = jnp.max(masked, axis=-1, keepdims=True)
    exponent = jnp.where(allowed, jnp.exp(masked - highest), 0.0)
    row_total = jnp.sum(exponent, axis=-1, keepdims=True)
    live_rows = row_total > 0.0
    safe_total = jnp.where(live_rows, row_total, 1.0)
    probability = (exponent / safe_total).astype(bf16)
    mixed = jnp.einsum("hqk,hkd->hqd", probability, value_heads, preferred_element_type=f32)
    merged = jnp.where(live_rows, highest + jnp.log(safe_total), 0.0)
    return mixed, merged


def attend_back(queries, key_heads, value_heads, grad_mixed, merged, allowed):
    scores = (
        jnp.einsum("hqd,hkd->hqk", queries, key_heads, preferred_element_type=f32) * HD ** (-0.5)
    )
    probability = jnp.where(allowed, jnp.exp(scores - merged), 0.0)
    grad_value_heads = jnp.einsum(
        "hqk,hqd->hkd", probability.astype(bf16), grad_mixed, preferred_element_type=f32
    )
    grad_prob = jnp.einsum("hqd,hkd->hqk", grad_mixed, value_heads, preferred_element_type=f32)
    row_delta = jnp.sum(probability * grad_prob, axis=-1, keepdims=True)
    grad_scores = (probability * (grad_prob - row_delta)).astype(bf16)
    grad_queries = jnp.einsum(
        "hqk,hkd->hqd", grad_scores, key_heads, preferred_element_type=f32
    ) * HD ** (-0.5)
    grad_key_heads = jnp.einsum(
        "hqk,hqd->hkd", grad_scores, queries, preferred_element_type=f32
    ) * HD ** (-0.5)
    return grad_queries, grad_key_heads, grad_value_heads


def local(
    tokens, doc_lengths, w_query, w_key, w_value, w_out, w_gate, w_up, w_down, norm_gains, cotangent
):
    plan = Plan()
    micro_count, sequences, half_rows, width = tokens.shape
    assert micro_count == 2 and sequences == 1
    quarter = half_rows // 2
    heads = w_query.shape[2] // HD
    n = plan.n
    group = 2 * plan.y + plan.x
    qw, kw = heads * HD, 2 * HD

    kv_at = plan.t * heads // GROUP_SIZE * HD
    hidden_units = w_gate.shape[2]
    attn_width = qw + 2 * kw + qw
    attn_shards = []
    for layer in range(LAYERS):
        keys = lax.dynamic_slice_in_dim(w_key[layer], kv_at, kw, axis=1)
        values = lax.dynamic_slice_in_dim(w_value[layer], kv_at, kw, axis=1)
        attn_shards += [w_query[layer], keys, values, w_out[layer].T]
    swapped = [plan.swap(jnp.concatenate(attn_shards, axis=1))]
    swapped[-1], w_gate, w_up, w_down, tokens, cotangent, norm_gains = lax.optimization_barrier(
        (swapped[-1], w_gate, w_up, w_down, tokens, cotangent, norm_gains)
    )
    for layer in range(LAYERS):
        shard = jnp.concatenate([w_gate[layer], w_up[layer], w_down[layer].T], axis=1)
        if layer:
            shard, swapped[-1] = lax.optimization_barrier((shard, swapped[-1]))
        swapped.append(plan.swap(shard))
    owned = []
    for index, shard in enumerate(swapped):
        if index > 1:
            shard, owned[-1] = lax.optimization_barrier((shard, owned[-1]))
        owned.append(lax.all_gather(shard, "dp", axis=0, tiled=True))

    def columns(halves, start, stop):
        return tuple(part[:, start:stop] for part in halves)

    def both_parities(own, after=None):
        if after is not None:
            own, after = lax.optimization_barrier((own, after))
        return (own, plan.core(own)), after

    side = lax.ppermute(norm_gains, "ctx", [(0, 1), (1, 0)])
    pair = jnp.where(
        plan.x == 0,
        jnp.concatenate([norm_gains, side], axis=1),
        jnp.concatenate([side, norm_gains], axis=1),
    )
    gain_pieces = [pair]
    for _ in range(1, n):
        gain_pieces.append(lax.ppermute(gain_pieces[-1], "dp", plan.down))
    ring = jnp.concatenate(gain_pieces + gain_pieces, axis=1)
    gain_width = pair.shape[1]
    gains = lax.dynamic_slice_in_dim(
        ring, (n - plan.z) % n * gain_width, n * gain_width, axis=1
    ).astype(f32)
    gain_attn = plan.inward(gains[:, :width])
    gain_ffn = plan.inward(gains[:, width : 2 * width])
    gain_query = gains[:, 2 * width : 2 * width + HD]
    gain_key = gains[:, 2 * width + HD :]

    blocks = jnp.arange(4, dtype=jnp.int32) ^ (2 * plan.x + plan.y).astype(jnp.int32)
    places = (blocks[:, None] * quarter + jnp.arange(quarter, dtype=jnp.int32)[None, :]).reshape(-1)
    lengths = lax.dynamic_index_in_dim(doc_lengths, plan.c, axis=0, keepdims=False)[0]
    docs = lengths.shape[0]
    ends = jnp.cumsum(lengths, dtype=jnp.int32)
    starts = ends - lengths
    document = jnp.sum((places[:, None] >= ends[None, :]).astype(jnp.int32), axis=-1)
    chosen = document[:, None] == jnp.arange(docs, dtype=jnp.int32)[None, :]
    position = places - jnp.sum(jnp.where(chosen, starts[None, :], 0), axis=-1)
    segment = jnp.where(document < docs, document, -1)
    allowed = (
        (segment[:, None] == segment[None, :])
        & (segment[:, None] >= 0)
        & (places[None, :] <= places[:, None])
    )[None]
    frequency = rope_base ** (-jnp.arange(HD // 2, dtype=f32) * (2.0 / HD))
    angle = position.astype(f32)[:, None] * frequency
    cosine, sine_value = jnp.cos(angle), jnp.sin(angle)
    pair_start = group * heads // GROUP_SIZE
    first_pair = (
        group * heads + jnp.arange(heads, dtype=jnp.int32)
    ) // GROUP_SIZE == pair_start
    weight_first = first_pair.astype(f32)[:, None, None]

    def own_half(array):
        rows = lax.dynamic_index_in_dim(array, plan.c, axis=0, keepdims=False)[0]
        rows = jnp.where(plan.y == 0, rows, jnp.roll(rows, quarter, axis=0))
        return plan.inward(rows)

    def by_head(array, count):
        return jnp.swapaxes(array.reshape(array.shape[0], count, HD), 0, 1)

    def flat(array):
        return jnp.swapaxes(array, 0, 1).reshape(array.shape[1], -1)

    first_half = own_half(tokens)
    cot_half = own_half(cotangent)
    cot_all = jnp.concatenate([cot_half, plan.peer(cot_half, 2)], axis=0)
    tokens_all = jnp.concatenate([first_half, plan.peer(first_half, 2)], axis=0).astype(f32)
    start_grad = jnp.where(segment[:, None] >= 0, cot_all, jnp.zeros_like(cot_all))

    state = tokens_all[:quarter]
    stored = []
    fetched = []
    attn_all, _ = both_parities(owned[0])
    for layer in range(LAYERS):
        attn_w = columns(attn_all, layer * attn_width, (layer + 1) * attn_width)
        w_qkv = columns(attn_w, 0, qw + 2 * kw)
        w_o = columns(attn_w, qw + 2 * kw, None)
        if layer == 0:
            scale_in = scale_of(tokens_all)
            normed = (tokens_all * scale_in * gain_attn[layer]).astype(bf16)
            normed, start_grad = lax.optimization_barrier((normed, start_grad))
            scale_in = scale_in[:quarter]
        else:
            scale_in = scale_of(state)
            normed = next_normed
        qkv = plan.into(normed, w_qkv)
        queries = by_head(qkv[:, :qw], heads)
        query_scale = scale_of(queries)
        query_low = rotate(queries * query_scale * gain_query[layer], cosine, sine_value).astype(
            bf16
        )
        keys = by_head(qkv[:, qw : qw + kw], 2)
        key_scale = scale_of(keys)
        key_low = rotate(keys * key_scale * gain_key[layer], cosine, sine_value).astype(bf16)
        value_low = by_head(qkv[:, qw + kw :].astype(bf16), 2)
        key_heads = jnp.where(first_pair[:, None, None], key_low[0][None], key_low[1][None])
        value_heads = jnp.where(first_pair[:, None, None], value_low[0][None], value_low[1][None])
        mixed, merged = attend(query_low, key_heads, value_heads, allowed)
        mixed_low = flat(mixed.astype(bf16))
        attn_terms = plan.out_of(mixed_low, w_o)
        middle, normed2 = join(attn_terms, state, gain_ffn[layer])
        ffn_w, later_middle = both_parities(owned[layer + 1], middle)
        w_g = columns(ffn_w, 0, hidden_units)
        w_u = columns(ffn_w, hidden_units, 2 * hidden_units)
        w_gu = columns(ffn_w, 0, 2 * hidden_units)
        scale_mid = scale_of(middle)
        gate = plan.into(normed2, w_g)
        up = plan.into(normed2, w_u)
        hidden = (jax.nn.silu(gate) * up).astype(bf16)
        w_d = columns(ffn_w, 2 * hidden_units, None)
        ffn_terms = plan.out_of(hidden, w_d)
        fetched.append((w_qkv, w_o, w_d, w_gu))
        stored.append(
            (
                state,
                scale_in,
                normed,
                queries,
                query_scale,
                query_low,
                keys,
                key_scale,
                key_heads,
                value_heads,
                merged,
                mixed_low,
                middle,
                scale_mid,
                normed2,
                gate,
                up,
                hidden,
            )
        )
        if layer + 1 < LAYERS:
            state, next_normed = join(ffn_terms, later_middle, gain_attn[layer + 1])

    gradient = start_grad[:quarter].astype(f32)
    grad_ffn = start_grad
    results = [[None] * 3 for _ in range(LAYERS)]
    last = []

    def finish(term):
        moved = plan.swap(term)
        keys = jnp.zeros((term.shape[0], w_key.shape[2]), f32)
        values = keys
        for j in range(plan.nt):
            part = moved[:, qw : qw + 2 * kw] if j == 0 else plan.cross(term[:, qw : qw + 2 * kw], j)
            part = part.astype(f32)
            sender = 2 * (plan.y ^ (j // 2)) + (plan.c ^ (j % 2))
            at = sender * heads // GROUP_SIZE * HD
            zeros = jnp.zeros_like(keys)
            keys += lax.dynamic_update_slice_in_dim(zeros, part[:, :kw], at, axis=1)
            values += lax.dynamic_update_slice_in_dim(zeros, part[:, kw:], at, axis=1)
        query = moved[:, :qw].astype(f32)
        out = moved[:, qw + 2 * kw :].T.astype(f32)
        return query, keys, values, out

    def scatter_next(layer, member, term):
        if len(last) > 1:
            at, part = last[-2]
            term, results[at][part] = lax.optimization_barrier((term, results[at][part]))
        results[layer][member] = plan.scatter(term)
        last.append((layer, member))

    gain_grads = [None] * LAYERS
    for layer in reversed(range(LAYERS)):
        w_qkv, w_o, w_d, w_gu = fetched[layer]
        (
            state,
            scale_in,
            normed,
            queries,
            query_scale,
            query_low,
            keys,
            key_scale,
            key_heads,
            value_heads,
            merged,
            mixed_low,
            middle,
            scale_mid,
            normed2,
            gate,
            up,
            hidden,
        ) = stored[layer]
        if grad_ffn is None:
            grad_ffn, results[layer + 1][1] = plan.spread_beside(
                gradient.astype(bf16), results[layer + 1][1]
            )
        term_d = plan.weight_term(grad_ffn, hidden)
        if layer + 1 == LAYERS:
            scatter_next(layer, 2, term_d)
        grad_hidden = plan.into(grad_ffn, w_d)
        sigmoid_gate = jax.nn.sigmoid(gate)
        grad_gate = (
            grad_hidden * up * sigmoid_gate * (1.0 + gate * (1.0 - sigmoid_gate))
        ).astype(bf16)
        grad_up = (grad_hidden * (gate * sigmoid_gate)).astype(bf16)
        grad_gu = jnp.concatenate([grad_gate, grad_up], axis=1)
        if layer + 1 < LAYERS:
            above = results[layer + 1]
            ffn_high = plan.swap(jnp.concatenate([above[1], above[2]], axis=1))
            grad_gu, ffn_high, above[0], term_d = lax.optimization_barrier(
                (grad_gu, ffn_high, above[0], term_d)
            )
        term_gu = plan.weight_term(normed2, grad_gu)
        mid_terms = plan.out_of(grad_gu, w_gu)
        if layer + 1 == LAYERS:
            summed_mid, term_gu = plan.gather_sum(mid_terms, term_gu)
        else:
            scatter_next(layer, 2, term_d)
            summed_mid, term_gu = plan.gather_sum(mid_terms, term_gu)
            summed_mid, results[layer][2] = lax.optimization_barrier(
                (summed_mid, results[layer][2])
            )
        scatter_next(layer, 1, term_gu)
        grad_g_ffn = jnp.sum(summed_mid * middle * scale_mid, axis=0)
        grad_mid = gradient + norm_back(summed_mid, middle, scale_mid, gain_ffn[layer])
        grad_attn = plan.spread(grad_mid.astype(bf16))
        grad_mixed = by_head(plan.into(grad_attn, w_o).astype(bf16), heads)
        term_o = plan.weight_term(grad_attn, mixed_low)
        grad_query_rot, grad_key_heads, grad_value_heads = attend_back(
            query_low, key_heads, value_heads, grad_mixed, merged, allowed
        )
        grad_key_rot = jnp.stack(
            [
                jnp.sum(grad_key_heads * weight_first, axis=0),
                jnp.sum(grad_key_heads * (1.0 - weight_first), axis=0),
            ]
        )
        grad_values = jnp.concatenate(
            [
                jnp.sum(grad_value_heads * weight_first, axis=0),
                jnp.sum(grad_value_heads * (1.0 - weight_first), axis=0),
            ],
            axis=1,
        ).astype(bf16)
        grad_query_norm = rotate(grad_query_rot, cosine, -sine_value)
        grad_g_query = jnp.sum(grad_query_norm * queries * query_scale, axis=(0, 1))
        grad_queries = flat(
            norm_back(grad_query_norm, queries, query_scale, gain_query[layer]).astype(bf16)
        )
        grad_key_norm = rotate(grad_key_rot, cosine, -sine_value)
        grad_g_key = jnp.sum(grad_key_norm * keys * key_scale, axis=(0, 1))
        grad_keys = flat(norm_back(grad_key_norm, keys, key_scale, gain_key[layer]).astype(bf16))
        grad_qkv = jnp.concatenate([grad_queries, grad_keys, grad_values], axis=1)
        if layer + 1 < LAYERS:
            attn_high = finish(results[layer + 1][0])
            grad_qkv, attn_high = lax.optimization_barrier((grad_qkv, attn_high))
        term_qkv = plan.weight_term(normed, grad_qkv)
        summed_in, (term_o, term_qkv) = plan.gather_sum(
            plan.out_of(grad_qkv, w_qkv), (term_o, term_qkv)
        )
        scatter_next(layer, 0, jnp.concatenate([term_qkv, term_o], axis=1))
        grad_g_attn = jnp.sum(summed_in * state * scale_in, axis=0)
        gradient = grad_mid + norm_back(summed_in, state, scale_in, gain_attn[layer])
        grad_ffn = None
        gain_grads[layer] = jnp.concatenate(
            [plan.outward(grad_g_attn), plan.outward(grad_g_ffn), grad_g_query, grad_g_key]
        )
    ffn_terms, gradient = lax.optimization_barrier((ffn_terms, gradient))
    ffn, _ = plan.gather_sum(ffn_terms)
    output = plan.both_quarters(plan.outward((later_middle + ffn).astype(bf16)))
    output = (output, plan.core(output))
    grad_input = plan.both_quarters(plan.outward(gradient.astype(bf16)))
    grad_input = (grad_input, plan.core(grad_input))
    all_gains = plan.total(jnp.stack(gain_grads))

    ffn_low = plan.swap(jnp.concatenate([results[0][1], results[0][2]], axis=1))
    grad_down = jnp.stack([ffn[:, 2 * hidden_units :].T for ffn in (ffn_low, ffn_high)])
    attn_low, ffn_low, grad_down, output, grad_input, all_gains = lax.optimization_barrier(
        (results[0][0], ffn_low, grad_down.astype(f32), output, grad_input, all_gains)
    )
    grad_gate = jnp.stack([ffn[:, :hidden_units] for ffn in (ffn_low, ffn_high)])
    grad_up = jnp.stack([ffn[:, hidden_units : 2 * hidden_units] for ffn in (ffn_low, ffn_high)])
    output = plan.both_micro(*output)
    grad_input = plan.both_micro(*grad_input).astype(f32)
    grad_query, grad_key, grad_value, grad_out = (
        jnp.stack(pair) for pair in zip(finish(attn_low), attn_high)
    )
    share = norm_gains.shape[1]
    grad_gains = lax.dynamic_slice_in_dim(
        all_gains, (2 * plan.z + plan.x) * share, share, axis=1
    )
    return (
        output[:, None],
        grad_input[:, None],
        grad_query,
        grad_key,
        grad_value,
        grad_out,
        grad_gate.astype(f32),
        grad_up.astype(f32),
        grad_down,
        grad_gains,
    )


def solution(mesh):
    placed = (
        P(None, "dp", "ctx", None),
        P(None, "dp", None),
        P(None, ("dp", "ctx"), "tensor"),
        P(None, ("dp", "ctx"), None),
        P(None, ("dp", "ctx"), None),
        P(None, "tensor", ("dp", "ctx")),
        P(None, ("dp", "ctx"), "tensor"),
        P(None, ("dp", "ctx"), "tensor"),
        P(None, "tensor", ("dp", "ctx")),
        P(None, ("dp", "ctx")),
        P(None, "dp", "ctx", None),
    )
    return jax.shard_map(
        local,
        mesh=mesh,
        in_specs=placed,
        out_specs=(
            P(None, "dp", "ctx", None),
            P(None, "dp", "ctx", None),
            P(None, ("dp", "ctx"), "tensor"),
            P(None, ("dp", "ctx"), None),
            P(None, ("dp", "ctx"), None),
            P(None, "tensor", ("dp", "ctx")),
            P(None, ("dp", "ctx"), "tensor"),
            P(None, ("dp", "ctx"), "tensor"),
            P(None, "tensor", ("dp", "ctx")),
            P(None, ("dp", "ctx")),
        ),
        check_vma=False,
    )
```

```python
import jax
import jax.numpy as jnp
from jax import lax
from jax.experimental import pallas as pl
from jax.experimental.pallas import tpu as pltpu
from jax.sharding import PartitionSpec as P

HQ = 20
HK = 5
HD = 64
LAYERS = 2
GROUP_SIZE = HQ // HK

epsilon = 1e-05
rope_base = 10000.0

f32 = jnp.float32
bf16 = jnp.bfloat16


def product(left_side, right_side, contract):
    return lax.dot_general(
        left_side, right_side, (contract, ((), ())), preferred_element_type=f32
    )


def rotate(values, cosine, sine_value):
    half_size = values.shape[-1] // 2
    first_half = values[..., :half_size]
    second_half = values[..., half_size:]
    return jnp.concatenate(
        [
            first_half * cosine - second_half * sine_value,
            second_half * cosine + first_half * sine_value,
        ],
        axis=-1,
    )


def scale_of(values):
    return lax.rsqrt(jnp.mean(values * values, axis=-1, keepdims=True) + epsilon)


def norm_back(gradient, values, scaling, gain_vector):
    scaled = gradient * gain_vector
    cubed = scaling * scaling * scaling
    return scaling * scaled - values * cubed * jnp.mean(scaled * values, axis=-1, keepdims=True)


PARTS = 2


def join_kernel(terms, state, gain, middle, normed, inbox, sum_send, sum_recv, row_send, row_recv):
    x, t = lax.axis_index("ctx"), lax.axis_index("tensor")
    other_x, other_t = 1 - x, t + 2 - 4 * (t // 2)
    peers = [
        {"ctx": x, "tensor": other_t},
        {"ctx": other_x, "tensor": t},
        {"ctx": other_x, "tensor": other_t},
    ]
    rows = state.shape[0]
    step = rows // PARTS
    barrier = pltpu.get_barrier_semaphore()
    for peer in peers:
        pl.semaphore_signal(barrier, inc=1, device_id=peer, device_id_type=pl.DeviceIdType.MESH)
    pl.semaphore_wait(barrier, len(peers))

    def sum_copy(part, j):
        return pltpu.make_async_remote_copy(
            src_ref=terms.at[pl.ds((j + 1) * rows + part * step, step)],
            dst_ref=inbox.at[part, j],
            send_sem=sum_send.at[part, j],
            recv_sem=sum_recv.at[part, j],
            device_id=peers[j],
            device_id_type=pl.DeviceIdType.MESH,
        )

    def row_copy(part, j):
        return pltpu.make_async_remote_copy(
            src_ref=normed.at[pl.ds(part * step, step)],
            dst_ref=normed.at[pl.ds((j + 1) * rows + part * step, step)],
            send_sem=row_send.at[part, j],
            recv_sem=row_recv.at[part, j],
            device_id=peers[j],
            device_id_type=pl.DeviceIdType.MESH,
        )

    for part in range(PARTS):
        for j in (2, 1, 0):
            sum_copy(part, j).start()
    for part in range(PARTS):
        here = pl.ds(part * step, step)
        total = terms[here].astype(f32)
        for j in range(3):
            sum_copy(part, j).wait_recv()
            total = total + inbox[part, j].astype(f32)
        total = state[here] + total
        middle[here] = total
        normed[here] = (total * scale_of(total) * gain[...]).astype(bf16)
        for j in (2, 1, 0):
            row_copy(part, j).start()
    for part in range(PARTS):
        for j in range(3):
            sum_copy(part, j).wait_send()
            row_copy(part, j).wait_send()
            row_copy(part, j).wait_recv()


def join(terms, state, gain):
    rows, width = state.shape
    whole = pl.BlockSpec(memory_space=pltpu.VMEM)
    return pl.pallas_call(
        join_kernel,
        out_shape=(
            jax.ShapeDtypeStruct((rows, width), f32),
            jax.ShapeDtypeStruct((4 * rows, width), bf16),
        ),
        in_specs=[whole] * 3,
        out_specs=(whole, whole),
        scratch_shapes=[pltpu.VMEM((PARTS, 3, rows // PARTS, width), bf16)]
        + [pltpu.SemaphoreType.DMA((PARTS, 3))] * 4,
        compiler_params=pltpu.CompilerParams(
            collective_id=0, has_side_effects=True, vmem_limit_bytes=32 * 2**20
        ),
        cost_estimate=pl.CostEstimate(flops=1000, bytes_accessed=1000, transcendentals=0),
        name="join",
    )(terms, state, gain[None])


class Plan:
    def __init__(self):
        self.n = lax.axis_size("dp")
        self.nt = lax.axis_size("tensor")
        assert lax.axis_size("ctx") == 2 and self.nt == 4
        self.z = lax.axis_index("dp")
        self.x = lax.axis_index("ctx")
        self.t = lax.axis_index("tensor")
        self.y = self.t // 2
        self.c = self.t % 2
        nt = self.nt
        places = [(a, b, d) for a in range(2) for b in range(2) for d in range(2)]
        self.peers = {}
        for j in range(1, 4):
            self.peers[j] = [
                (a * nt + 2 * b + d, (a ^ (j // 2)) * nt + 2 * (b ^ (j % 2)) + d)
                for a, b, d in places
            ]
        self.swap_pairs = [
            (a * nt + 2 * b + d, d * nt + 2 * b + a) for a, b, d in places if a != d
        ]
        self.cross_pairs = {
            j: [
                (a * nt + 2 * b + d, d * nt + 2 * (b ^ (j // 2)) + (a ^ (j % 2)))
                for a, b, d in places
            ]
            for j in range(1, 4)
        }
        assert self.n & (self.n - 1) == 0
        self.core_all = [(i, i ^ 1) for i in range(2 * nt)]
        self.core_pairs = [(i, i ^ 1) for i in range(nt)]
        self.up = [(i, (i + 1) % self.n) for i in range(self.n)]
        self.down = [(i, (i - 1) % self.n) for i in range(self.n)]

    def peer(self, value, j):
        return lax.ppermute(value, ("ctx", "tensor"), self.peers[j])

    def swap(self, value):
        moved = lax.ppermute(value, ("ctx", "tensor"), self.swap_pairs)
        return jnp.where(self.x == self.c, value, moved)

    def cross(self, value, j):
        return lax.ppermute(value, ("ctx", "tensor"), self.cross_pairs[j])

    def core(self, value):
        return lax.ppermute(value, "tensor", self.core_pairs)

    def total(self, value):
        for pairs in self.peers[1], self.peers[2], self.core_all:
            value = value + lax.ppermute(value, ("ctx", "tensor"), pairs)
        step = 1
        while step < self.n:
            value = value + lax.ppermute(value, "dp", [(i, i ^ step) for i in range(self.n)])
            step *= 2
        return value

    def weight_term(self, left, right):
        half = left.shape[1] // 2
        away = self.core(product(left[:, half:], right, ((0,), (0,))).astype(bf16))
        return (product(left[:, :half], right, ((0,), (0,))) + away.astype(f32)).astype(bf16)

    def scatter(self, term):
        return lax.psum_scatter(term, "dp", scatter_dimension=0, tiled=True)

    def into(self, rows, halves):
        half = rows.shape[1] // 2
        return product(rows[:, :half], halves[0], ((1,), (0,))) + product(
            rows[:, half:], halves[1], ((1,), (0,))
        )

    def out_of(self, rows, halves):
        return jnp.concatenate(
            [product(rows, part, ((1,), (1,))).astype(bf16) for part in halves], axis=1
        )

    def spread(self, rows):
        return jnp.concatenate([rows] + [self.peer(rows, j) for j in range(1, 4)], axis=0)

    def spread_beside(self, rows, beside):
        moved = [self.peer(rows, j) for j in range(1, 4)]
        moved, beside = lax.optimization_barrier((moved, beside))
        return jnp.concatenate([rows] + moved, axis=0), beside

    def gather_sum(self, terms, beside=()):
        rows = terms.shape[0] // 4
        moved = [self.peer(terms[j * rows : (j + 1) * rows], j) for j in range(1, 4)]
        moved, beside = lax.optimization_barrier((moved, beside))
        total = terms[:rows].astype(f32)
        for piece in moved:
            total = total + piece.astype(f32)
        return total, beside

    def inward(self, array):
        lead = array.shape[:-1]
        d = array.shape[-1]
        w = d // (2 * self.n)
        parts = array.reshape(lead + (self.n, 2, w))
        even = parts[..., 0, :].reshape(lead + (d // 2,))
        odd = parts[..., 1, :].reshape(lead + (d // 2,))
        return jnp.where(
            self.c == 0,
            jnp.concatenate([even, odd], axis=-1),
            jnp.concatenate([odd, even], axis=-1),
        )

    def outward(self, array):
        w = array.shape[-1] // (2 * self.n)
        parts = [array[..., i * w : (i + 1) * w] for i in range(2 * self.n)]
        pairs = list(zip(parts[: self.n], parts[self.n :]))
        return jnp.where(
            self.c == 0,
            jnp.concatenate([part for pair in pairs for part in pair], axis=-1),
            jnp.concatenate([part for pair in pairs for part in pair[::-1]], axis=-1),
        )

    def both_quarters(self, rows):
        beside = self.peer(rows, 1)
        return jnp.where(
            self.y == 0,
            jnp.concatenate([rows, beside], axis=0),
            jnp.concatenate([beside, rows], axis=0),
        )

    def both_micro(self, half, other):
        return jnp.where(self.c == 0, jnp.stack([half, other]), jnp.stack([other, half]))


def attend(queries, key_heads, value_heads, allowed):
    scores = (
        jnp.einsum("hqd,hkd->hqk", queries, key_heads, preferred_element_type=f32) * HD ** (-0.5)
    )
    masked = jnp.where(allowed, scores, -1e30)
    highest = jnp.max(masked, axis=-1, keepdims=True)
    exponent = jnp.where(allowed, jnp.exp(masked - highest), 0.0)
    row_total = jnp.sum(exponent, axis=-1, keepdims=True)
    live_rows = row_total > 0.0
    safe_total = jnp.where(live_rows, row_total, 1.0)
    probability = (exponent / safe_total).astype(bf16)
    mixed = jnp.einsum("hqk,hkd->hqd", probability, value_heads, preferred_element_type=f32)
    merged = jnp.where(live_rows, highest + jnp.log(safe_total), 0.0)
    return mixed, merged


def attend_back(queries, key_heads, value_heads, grad_mixed, merged, allowed):
    scores = (
        jnp.einsum("hqd,hkd->hqk", queries, key_heads, preferred_element_type=f32) * HD ** (-0.5)
    )
    probability = jnp.where(allowed, jnp.exp(scores - merged), 0.0)
    grad_value_heads = jnp.einsum(
        "hqk,hqd->hkd", probability.astype(bf16), grad_mixed, preferred_element_type=f32
    )
    grad_prob = jnp.einsum("hqd,hkd->hqk", grad_mixed, value_heads, preferred_element_type=f32)
    row_delta = jnp.sum(probability * grad_prob, axis=-1, keepdims=True)
    grad_scores = (probability * (grad_prob - row_delta)).astype(bf16)
    grad_queries = jnp.einsum(
        "hqk,hkd->hqd", grad_scores, key_heads, preferred_element_type=f32
    ) * HD ** (-0.5)
    grad_key_heads = jnp.einsum(
        "hqk,hqd->hkd", grad_scores, queries, preferred_element_type=f32
    ) * HD ** (-0.5)
    return grad_queries, grad_key_heads, grad_value_heads


def local(
    tokens, doc_lengths, w_query, w_key, w_value, w_out, w_gate, w_up, w_down, norm_gains, cotangent
):
    plan = Plan()
    micro_count, sequences, half_rows, width = tokens.shape
    assert micro_count == 2 and sequences == 1
    quarter = half_rows // 2
    heads = w_query.shape[2] // HD
    n = plan.n
    group = 2 * plan.y + plan.x
    qw, kw = heads * HD, 2 * HD

    kv_at = plan.t * heads // GROUP_SIZE * HD
    hidden_units = w_gate.shape[2]
    attn_width = qw + 2 * kw + qw
    attn_shards = []
    for layer in range(LAYERS):
        keys = lax.dynamic_slice_in_dim(w_key[layer], kv_at, kw, axis=1)
        values = lax.dynamic_slice_in_dim(w_value[layer], kv_at, kw, axis=1)
        attn_shards += [w_query[layer], keys, values, w_out[layer].T]
    swapped = [plan.swap(jnp.concatenate(attn_shards, axis=1))]
    swapped[-1], w_gate, w_up, w_down, tokens, cotangent, norm_gains = lax.optimization_barrier(
        (swapped[-1], w_gate, w_up, w_down, tokens, cotangent, norm_gains)
    )
    for layer in range(LAYERS):
        shard = jnp.concatenate([w_gate[layer], w_up[layer], w_down[layer].T], axis=1)
        if layer:
            shard, swapped[-1] = lax.optimization_barrier((shard, swapped[-1]))
        swapped.append(plan.swap(shard))
    owned = []
    for index, shard in enumerate(swapped):
        if index > 1:
            shard, owned[-1] = lax.optimization_barrier((shard, owned[-1]))
        owned.append(lax.all_gather(shard, "dp", axis=0, tiled=True))

    def columns(halves, start, stop):
        return tuple(part[:, start:stop] for part in halves)

    def both_parities(own, after=None):
        if after is not None:
            own, after = lax.optimization_barrier((own, after))
        return (own, plan.core(own)), after

    side = lax.ppermute(norm_gains, "ctx", [(0, 1), (1, 0)])
    pair = jnp.where(
        plan.x == 0,
        jnp.concatenate([norm_gains, side], axis=1),
        jnp.concatenate([side, norm_gains], axis=1),
    )
    gain_pieces = [pair]
    for _ in range(1, n):
        gain_pieces.append(lax.ppermute(gain_pieces[-1], "dp", plan.down))
    ring = jnp.concatenate(gain_pieces + gain_pieces, axis=1)
    gain_width = pair.shape[1]
    gains = lax.dynamic_slice_in_dim(
        ring, (n - plan.z) % n * gain_width, n * gain_width, axis=1
    ).astype(f32)
    gain_attn = plan.inward(gains[:, :width])
    gain_ffn = plan.inward(gains[:, width : 2 * width])
    gain_query = gains[:, 2 * width : 2 * width + HD]
    gain_key = gains[:, 2 * width + HD :]

    blocks = jnp.arange(4, dtype=jnp.int32) ^ (2 * plan.x + plan.y).astype(jnp.int32)
    places = (blocks[:, None] * quarter + jnp.arange(quarter, dtype=jnp.int32)[None, :]).reshape(-1)
    lengths = lax.dynamic_index_in_dim(doc_lengths, plan.c, axis=0, keepdims=False)[0]
    docs = lengths.shape[0]
    ends = jnp.cumsum(lengths, dtype=jnp.int32)
    starts = ends - lengths
    document = jnp.sum((places[:, None] >= ends[None, :]).astype(jnp.int32), axis=-1)
    chosen = document[:, None] == jnp.arange(docs, dtype=jnp.int32)[None, :]
    position = places - jnp.sum(jnp.where(chosen, starts[None, :], 0), axis=-1)
    segment = jnp.where(document < docs, document, -1)
    allowed = (
        (segment[:, None] == segment[None, :])
        & (segment[:, None] >= 0)
        & (places[None, :] <= places[:, None])
    )[None]
    frequency = rope_base ** (-jnp.arange(HD // 2, dtype=f32) * (2.0 / HD))
    angle = position.astype(f32)[:, None] * frequency
    cosine, sine_value = jnp.cos(angle), jnp.sin(angle)
    pair_start = group * heads // GROUP_SIZE
    first_pair = (
        group * heads + jnp.arange(heads, dtype=jnp.int32)
    ) // GROUP_SIZE == pair_start
    weight_first = first_pair.astype(f32)[:, None, None]

    def own_half(array):
        rows = lax.dynamic_index_in_dim(array, plan.c, axis=0, keepdims=False)[0]
        rows = jnp.where(plan.y == 0, rows, jnp.roll(rows, quarter, axis=0))
        return plan.inward(rows)

    def by_head(array, count):
        return jnp.swapaxes(array.reshape(array.shape[0], count, HD), 0, 1)

    def flat(array):
        return jnp.swapaxes(array, 0, 1).reshape(array.shape[1], -1)

    first_half = own_half(tokens)
    cot_half = own_half(cotangent)
    cot_all = jnp.concatenate([cot_half, plan.peer(cot_half, 2)], axis=0)
    tokens_all = jnp.concatenate([first_half, plan.peer(first_half, 2)], axis=0).astype(f32)
    start_grad = jnp.where(segment[:, None] >= 0, cot_all, jnp.zeros_like(cot_all))

    state = tokens_all[:quarter]
    stored = []
    fetched = []
    attn_all, _ = both_parities(owned[0])
    for layer in range(LAYERS):
        attn_w = columns(attn_all, layer * attn_width, (layer + 1) * attn_width)
        w_qkv = columns(attn_w, 0, qw + 2 * kw)
        w_o = columns(attn_w, qw + 2 * kw, None)
        if layer == 0:
            scale_in = scale_of(tokens_all)
            normed = (tokens_all * scale_in * gain_attn[layer]).astype(bf16)
            normed, start_grad = lax.optimization_barrier((normed, start_grad))
            scale_in = scale_in[:quarter]
        else:
            scale_in = scale_of(state)
            normed = next_normed
        qkv = plan.into(normed, w_qkv)
        queries = by_head(qkv[:, :qw], heads)
        query_scale = scale_of(queries)
        query_low = rotate(queries * query_scale * gain_query[layer], cosine, sine_value).astype(
            bf16
        )
        keys = by_head(qkv[:, qw : qw + kw], 2)
        key_scale = scale_of(keys)
        key_low = rotate(keys * key_scale * gain_key[layer], cosine, sine_value).astype(bf16)
        value_low = by_head(qkv[:, qw + kw :].astype(bf16), 2)
        key_heads = jnp.where(first_pair[:, None, None], key_low[0][None], key_low[1][None])
        value_heads = jnp.where(first_pair[:, None, None], value_low[0][None], value_low[1][None])
        mixed, merged = attend(query_low, key_heads, value_heads, allowed)
        mixed_low = flat(mixed.astype(bf16))
        attn_terms = plan.out_of(mixed_low, w_o)
        middle, normed2 = join(attn_terms, state, gain_ffn[layer])
        ffn_w, later_middle = both_parities(owned[layer + 1], middle)
        w_g = columns(ffn_w, 0, hidden_units)
        w_u = columns(ffn_w, hidden_units, 2 * hidden_units)
        w_gu = columns(ffn_w, 0, 2 * hidden_units)
        scale_mid = scale_of(middle)
        gate = plan.into(normed2, w_g)
        up = plan.into(normed2, w_u)
        hidden = (jax.nn.silu(gate) * up).astype(bf16)
        w_d = columns(ffn_w, 2 * hidden_units, None)
        ffn_terms = plan.out_of(hidden, w_d)
        fetched.append((w_qkv, w_o, w_d, w_gu))
        stored.append(
            (
                state,
                scale_in,
                normed,
                queries,
                query_scale,
                query_low,
                keys,
                key_scale,
                key_heads,
                value_heads,
                merged,
                mixed_low,
                middle,
                scale_mid,
                normed2,
                gate,
                up,
                hidden,
            )
        )
        if layer + 1 < LAYERS:
            state, next_normed = join(ffn_terms, later_middle, gain_attn[layer + 1])

    gradient = start_grad[:quarter].astype(f32)
    grad_ffn = start_grad
    results = [[None] * 3 for _ in range(LAYERS)]
    last = []

    def finish(term):
        moved = plan.swap(term)
        keys = jnp.zeros((term.shape[0], w_key.shape[2]), f32)
        values = keys
        for j in range(plan.nt):
            part = moved[:, qw : qw + 2 * kw] if j == 0 else plan.cross(term[:, qw : qw + 2 * kw], j)
            part = part.astype(f32)
            sender = 2 * (plan.y ^ (j // 2)) + (plan.c ^ (j % 2))
            at = sender * heads // GROUP_SIZE * HD
            zeros = jnp.zeros_like(keys)
            keys += lax.dynamic_update_slice_in_dim(zeros, part[:, :kw], at, axis=1)
            values += lax.dynamic_update_slice_in_dim(zeros, part[:, kw:], at, axis=1)
        query = moved[:, :qw].astype(f32)
        out = moved[:, qw + 2 * kw :].T.astype(f32)
        return query, keys, values, out

    def scatter_next(layer, member, term):
        if len(last) > 1:
            at, part = last[-2]
            term, results[at][part] = lax.optimization_barrier((term, results[at][part]))
        results[layer][member] = plan.scatter(term)
        last.append((layer, member))

    gain_grads = [None] * LAYERS
    for layer in reversed(range(LAYERS)):
        w_qkv, w_o, w_d, w_gu = fetched[layer]
        (
            state,
            scale_in,
            normed,
            queries,
            query_scale,
            query_low,
            keys,
            key_scale,
            key_heads,
            value_heads,
            merged,
            mixed_low,
            middle,
            scale_mid,
            normed2,
            gate,
            up,
            hidden,
        ) = stored[layer]
        if grad_ffn is None:
            grad_ffn, results[layer + 1][1] = plan.spread_beside(
                gradient.astype(bf16), results[layer + 1][1]
            )
        term_d = plan.weight_term(grad_ffn, hidden)
        if layer + 1 == LAYERS:
            scatter_next(layer, 2, term_d)
        grad_hidden = plan.into(grad_ffn, w_d)
        sigmoid_gate = jax.nn.sigmoid(gate)
        grad_gate = (
            grad_hidden * up * sigmoid_gate * (1.0 + gate * (1.0 - sigmoid_gate))
        ).astype(bf16)
        grad_up = (grad_hidden * (gate * sigmoid_gate)).astype(bf16)
        grad_gu = jnp.concatenate([grad_gate, grad_up], axis=1)
        if layer + 1 < LAYERS:
            above = results[layer + 1]
            ffn_high = plan.swap(jnp.concatenate([above[1], above[2]], axis=1))
            grad_gu, ffn_high, term_d = lax.optimization_barrier((grad_gu, ffn_high, term_d))
        term_gu = plan.weight_term(normed2, grad_gu)
        mid_terms = plan.out_of(grad_gu, w_gu)
        if layer + 1 == LAYERS:
            summed_mid, term_gu = plan.gather_sum(mid_terms, term_gu)
        else:
            mid_terms, above[0] = lax.optimization_barrier((mid_terms, above[0]))
            scatter_next(layer, 2, term_d)
            summed_mid, term_gu = plan.gather_sum(mid_terms, term_gu)
            summed_mid, results[layer][2] = lax.optimization_barrier(
                (summed_mid, results[layer][2])
            )
        scatter_next(layer, 1, term_gu)
        grad_g_ffn = jnp.sum(summed_mid * middle * scale_mid, axis=0)
        grad_mid = gradient + norm_back(summed_mid, middle, scale_mid, gain_ffn[layer])
        grad_attn = plan.spread(grad_mid.astype(bf16))
        grad_mixed = by_head(plan.into(grad_attn, w_o).astype(bf16), heads)
        term_o = plan.weight_term(grad_attn, mixed_low)
        grad_query_rot, grad_key_heads, grad_value_heads = attend_back(
            query_low, key_heads, value_heads, grad_mixed, merged, allowed
        )
        grad_key_rot = jnp.stack(
            [
                jnp.sum(grad_key_heads * weight_first, axis=0),
                jnp.sum(grad_key_heads * (1.0 - weight_first), axis=0),
            ]
        )
        grad_values = jnp.concatenate(
            [
                jnp.sum(grad_value_heads * weight_first, axis=0),
                jnp.sum(grad_value_heads * (1.0 - weight_first), axis=0),
            ],
            axis=1,
        ).astype(bf16)
        grad_query_norm = rotate(grad_query_rot, cosine, -sine_value)
        grad_g_query = jnp.sum(grad_query_norm * queries * query_scale, axis=(0, 1))
        grad_queries = flat(
            norm_back(grad_query_norm, queries, query_scale, gain_query[layer]).astype(bf16)
        )
        grad_key_norm = rotate(grad_key_rot, cosine, -sine_value)
        grad_g_key = jnp.sum(grad_key_norm * keys * key_scale, axis=(0, 1))
        grad_keys = flat(norm_back(grad_key_norm, keys, key_scale, gain_key[layer]).astype(bf16))
        grad_qkv = jnp.concatenate([grad_queries, grad_keys, grad_values], axis=1)
        if layer + 1 < LAYERS:
            attn_high = finish(results[layer + 1][0])
            grad_qkv, attn_high = lax.optimization_barrier((grad_qkv, attn_high))
        term_qkv = plan.weight_term(normed, grad_qkv)
        summed_in, (term_o, term_qkv) = plan.gather_sum(
            plan.out_of(grad_qkv, w_qkv), (term_o, term_qkv)
        )
        scatter_next(layer, 0, jnp.concatenate([term_qkv, term_o], axis=1))
        grad_g_attn = jnp.sum(summed_in * state * scale_in, axis=0)
        gradient = grad_mid + norm_back(summed_in, state, scale_in, gain_attn[layer])
        grad_ffn = None
        gain_grads[layer] = jnp.concatenate(
            [plan.outward(grad_g_attn), plan.outward(grad_g_ffn), grad_g_query, grad_g_key]
        )
    ffn_terms, gradient = lax.optimization_barrier((ffn_terms, gradient))
    ffn, _ = plan.gather_sum(ffn_terms)
    output = plan.both_quarters(plan.outward((later_middle + ffn).astype(bf16)))
    output = (output, plan.core(output))
    grad_input = plan.both_quarters(plan.outward(gradient.astype(bf16)))
    grad_input = (grad_input, plan.core(grad_input))
    all_gains = plan.total(jnp.stack(gain_grads))

    ffn_low = plan.swap(jnp.concatenate([results[0][1], results[0][2]], axis=1))
    grad_down = jnp.stack([ffn[:, 2 * hidden_units :].T for ffn in (ffn_low, ffn_high)])
    attn_low, ffn_low, grad_down, output, grad_input, all_gains = lax.optimization_barrier(
        (results[0][0], ffn_low, grad_down.astype(f32), output, grad_input, all_gains)
    )
    grad_gate = jnp.stack([ffn[:, :hidden_units] for ffn in (ffn_low, ffn_high)])
    grad_up = jnp.stack([ffn[:, hidden_units : 2 * hidden_units] for ffn in (ffn_low, ffn_high)])
    output = plan.both_micro(*output)
    grad_input = plan.both_micro(*grad_input).astype(f32)
    grad_query, grad_key, grad_value, grad_out = (
        jnp.stack(pair) for pair in zip(finish(attn_low), attn_high)
    )
    share = norm_gains.shape[1]
    grad_gains = lax.dynamic_slice_in_dim(
        all_gains, (2 * plan.z + plan.x) * share, share, axis=1
    )
    return (
        output[:, None],
        grad_input[:, None],
        grad_query,
        grad_key,
        grad_value,
        grad_out,
        grad_gate.astype(f32),
        grad_up.astype(f32),
        grad_down,
        grad_gains,
    )


def solution(mesh):
    placed = (
        P(None, "dp", "ctx", None),
        P(None, "dp", None),
        P(None, ("dp", "ctx"), "tensor"),
        P(None, ("dp", "ctx"), None),
        P(None, ("dp", "ctx"), None),
        P(None, "tensor", ("dp", "ctx")),
        P(None, ("dp", "ctx"), "tensor"),
        P(None, ("dp", "ctx"), "tensor"),
        P(None, "tensor", ("dp", "ctx")),
        P(None, ("dp", "ctx")),
        P(None, "dp", "ctx", None),
    )
    return jax.shard_map(
        local,
        mesh=mesh,
        in_specs=placed,
        out_specs=(
            P(None, "dp", "ctx", None),
            P(None, "dp", "ctx", None),
            P(None, ("dp", "ctx"), "tensor"),
            P(None, ("dp", "ctx"), None),
            P(None, ("dp", "ctx"), None),
            P(None, "tensor", ("dp", "ctx")),
            P(None, ("dp", "ctx"), "tensor"),
            P(None, ("dp", "ctx"), "tensor"),
            P(None, "tensor", ("dp", "ctx")),
            P(None, ("dp", "ctx")),
        ),
        check_vma=False,
    )
```

```python
import jax
import jax.numpy as jnp
from jax import lax
from jax.experimental import pallas as pl
from jax.experimental.pallas import tpu as pltpu
from jax.sharding import PartitionSpec as P

HQ = 20
HK = 5
HD = 64
LAYERS = 2
GROUP_SIZE = HQ // HK

epsilon = 1e-05
rope_base = 10000.0

f32 = jnp.float32
bf16 = jnp.bfloat16


def product(left_side, right_side, contract):
    return lax.dot_general(
        left_side, right_side, (contract, ((), ())), preferred_element_type=f32
    )


def rotate(values, cosine, sine_value):
    half_size = values.shape[-1] // 2
    first_half = values[..., :half_size]
    second_half = values[..., half_size:]
    return jnp.concatenate(
        [
            first_half * cosine - second_half * sine_value,
            second_half * cosine + first_half * sine_value,
        ],
        axis=-1,
    )


def scale_of(values):
    return lax.rsqrt(jnp.mean(values * values, axis=-1, keepdims=True) + epsilon)


def norm_back(gradient, values, scaling, gain_vector):
    scaled = gradient * gain_vector
    cubed = scaling * scaling * scaling
    return scaling * scaled - values * cubed * jnp.mean(scaled * values, axis=-1, keepdims=True)


PARTS = 2


def join_kernel(terms, state, gain, middle, normed, inbox, sum_send, sum_recv, row_send, row_recv):
    x, t = lax.axis_index("ctx"), lax.axis_index("tensor")
    other_x, other_t = 1 - x, t + 2 - 4 * (t // 2)
    peers = [
        {"ctx": x, "tensor": other_t},
        {"ctx": other_x, "tensor": t},
        {"ctx": other_x, "tensor": other_t},
    ]
    rows = state.shape[0]
    step = rows // PARTS
    barrier = pltpu.get_barrier_semaphore()
    for peer in peers:
        pl.semaphore_signal(barrier, inc=1, device_id=peer, device_id_type=pl.DeviceIdType.MESH)
    pl.semaphore_wait(barrier, len(peers))

    def sum_copy(part, j):
        return pltpu.make_async_remote_copy(
            src_ref=terms.at[pl.ds((j + 1) * rows + part * step, step)],
            dst_ref=inbox.at[part, j],
            send_sem=sum_send.at[part, j],
            recv_sem=sum_recv.at[part, j],
            device_id=peers[j],
            device_id_type=pl.DeviceIdType.MESH,
        )

    def row_copy(part, j):
        return pltpu.make_async_remote_copy(
            src_ref=normed.at[pl.ds(part * step, step)],
            dst_ref=normed.at[pl.ds((j + 1) * rows + part * step, step)],
            send_sem=row_send.at[part, j],
            recv_sem=row_recv.at[part, j],
            device_id=peers[j],
            device_id_type=pl.DeviceIdType.MESH,
        )

    for part in range(PARTS):
        for j in (2, 1, 0):
            sum_copy(part, j).start()
    for part in range(PARTS):
        here = pl.ds(part * step, step)
        total = terms[here].astype(f32)
        for j in range(3):
            sum_copy(part, j).wait_recv()
            total = total + inbox[part, j].astype(f32)
        total = state[here] + total
        middle[here] = total
        normed[here] = (total * scale_of(total) * gain[...]).astype(bf16)
        for j in (2, 1, 0):
            row_copy(part, j).start()
    for part in range(PARTS):
        for j in range(3):
            sum_copy(part, j).wait_send()
            row_copy(part, j).wait_send()
            row_copy(part, j).wait_recv()


def join(terms, state, gain):
    rows, width = state.shape
    whole = pl.BlockSpec(memory_space=pltpu.VMEM)
    return pl.pallas_call(
        join_kernel,
        out_shape=(
            jax.ShapeDtypeStruct((rows, width), f32),
            jax.ShapeDtypeStruct((4 * rows, width), bf16),
        ),
        in_specs=[whole] * 3,
        out_specs=(whole, whole),
        scratch_shapes=[pltpu.VMEM((PARTS, 3, rows // PARTS, width), bf16)]
        + [pltpu.SemaphoreType.DMA((PARTS, 3))] * 4,
        compiler_params=pltpu.CompilerParams(
            collective_id=0, has_side_effects=True, vmem_limit_bytes=32 * 2**20
        ),
        cost_estimate=pl.CostEstimate(flops=1000, bytes_accessed=1000, transcendentals=0),
        name="join",
    )(terms, state, gain[None])


class Plan:
    def __init__(self):
        self.n = lax.axis_size("dp")
        self.nt = lax.axis_size("tensor")
        assert lax.axis_size("ctx") == 2 and self.nt == 4
        self.z = lax.axis_index("dp")
        self.x = lax.axis_index("ctx")
        self.t = lax.axis_index("tensor")
        self.y = self.t // 2
        self.c = self.t % 2
        nt = self.nt
        places = [(a, b, d) for a in range(2) for b in range(2) for d in range(2)]
        self.peers = {}
        for j in range(1, 4):
            self.peers[j] = [
                (a * nt + 2 * b + d, (a ^ (j // 2)) * nt + 2 * (b ^ (j % 2)) + d)
                for a, b, d in places
            ]
        self.swap_pairs = [
            (a * nt + 2 * b + d, d * nt + 2 * b + a) for a, b, d in places if a != d
        ]
        self.cross_pairs = {
            j: [
                (a * nt + 2 * b + d, d * nt + 2 * (b ^ (j // 2)) + (a ^ (j % 2)))
                for a, b, d in places
            ]
            for j in range(1, 4)
        }
        assert self.n & (self.n - 1) == 0
        self.core_all = [(i, i ^ 1) for i in range(2 * nt)]
        self.core_pairs = [(i, i ^ 1) for i in range(nt)]
        self.up = [(i, (i + 1) % self.n) for i in range(self.n)]
        self.down = [(i, (i - 1) % self.n) for i in range(self.n)]

    def peer(self, value, j):
        return lax.ppermute(value, ("ctx", "tensor"), self.peers[j])

    def swap(self, value):
        moved = lax.ppermute(value, ("ctx", "tensor"), self.swap_pairs)
        return jnp.where(self.x == self.c, value, moved)

    def cross(self, value, j):
        return lax.ppermute(value, ("ctx", "tensor"), self.cross_pairs[j])

    def core(self, value):
        return lax.ppermute(value, "tensor", self.core_pairs)

    def total(self, value):
        for pairs in self.peers[1], self.peers[2], self.core_all:
            value = value + lax.ppermute(value, ("ctx", "tensor"), pairs)
        step = 1
        while step < self.n:
            value = value + lax.ppermute(value, "dp", [(i, i ^ step) for i in range(self.n)])
            step *= 2
        return value

    def weight_term(self, left, right):
        half = left.shape[1] // 2
        away = self.core(product(left[:, half:], right, ((0,), (0,))).astype(bf16))
        return (product(left[:, :half], right, ((0,), (0,))) + away.astype(f32)).astype(bf16)

    def scatter(self, term):
        return lax.psum_scatter(term, "dp", scatter_dimension=0, tiled=True)

    def into(self, rows, halves):
        half = rows.shape[1] // 2
        return product(rows[:, :half], halves[0], ((1,), (0,))) + product(
            rows[:, half:], halves[1], ((1,), (0,))
        )

    def out_of(self, rows, halves):
        return jnp.concatenate(
            [product(rows, part, ((1,), (1,))).astype(bf16) for part in halves], axis=1
        )

    def spread(self, rows):
        return jnp.concatenate([rows] + [self.peer(rows, j) for j in range(1, 4)], axis=0)

    def spread_beside(self, rows, beside):
        moved = [self.peer(rows, j) for j in range(1, 4)]
        moved, beside = lax.optimization_barrier((moved, beside))
        return jnp.concatenate([rows] + moved, axis=0), beside

    def gather_sum(self, terms, beside=()):
        rows = terms.shape[0] // 4
        moved = [self.peer(terms[j * rows : (j + 1) * rows], j) for j in range(1, 4)]
        moved, beside = lax.optimization_barrier((moved, beside))
        total = terms[:rows].astype(f32)
        for piece in moved:
            total = total + piece.astype(f32)
        return total, beside

    def inward(self, array):
        lead = array.shape[:-1]
        d = array.shape[-1]
        w = d // (2 * self.n)
        parts = array.reshape(lead + (self.n, 2, w))
        even = parts[..., 0, :].reshape(lead + (d // 2,))
        odd = parts[..., 1, :].reshape(lead + (d // 2,))
        return jnp.where(
            self.c == 0,
            jnp.concatenate([even, odd], axis=-1),
            jnp.concatenate([odd, even], axis=-1),
        )

    def outward(self, array):
        w = array.shape[-1] // (2 * self.n)
        parts = [array[..., i * w : (i + 1) * w] for i in range(2 * self.n)]
        pairs = list(zip(parts[: self.n], parts[self.n :]))
        return jnp.where(
            self.c == 0,
            jnp.concatenate([part for pair in pairs for part in pair], axis=-1),
            jnp.concatenate([part for pair in pairs for part in pair[::-1]], axis=-1),
        )

    def both_quarters(self, rows):
        beside = self.peer(rows, 1)
        return jnp.where(
            self.y == 0,
            jnp.concatenate([rows, beside], axis=0),
            jnp.concatenate([beside, rows], axis=0),
        )

    def both_micro(self, half, other):
        return jnp.where(self.c == 0, jnp.stack([half, other]), jnp.stack([other, half]))


def attend(queries, key_heads, value_heads, allowed):
    scores = (
        jnp.einsum("hqd,hkd->hqk", queries, key_heads, preferred_element_type=f32) * HD ** (-0.5)
    )
    masked = jnp.where(allowed, scores, -1e30)
    highest = jnp.max(masked, axis=-1, keepdims=True)
    exponent = jnp.where(allowed, jnp.exp(masked - highest), 0.0)
    row_total = jnp.sum(exponent, axis=-1, keepdims=True)
    live_rows = row_total > 0.0
    safe_total = jnp.where(live_rows, row_total, 1.0)
    probability = (exponent / safe_total).astype(bf16)
    mixed = jnp.einsum("hqk,hkd->hqd", probability, value_heads, preferred_element_type=f32)
    merged = jnp.where(live_rows, highest + jnp.log(safe_total), 0.0)
    return mixed, merged


def attend_back(queries, key_heads, value_heads, grad_mixed, merged, allowed):
    scores = (
        jnp.einsum("hqd,hkd->hqk", queries, key_heads, preferred_element_type=f32) * HD ** (-0.5)
    )
    probability = jnp.where(allowed, jnp.exp(scores - merged), 0.0)
    grad_value_heads = jnp.einsum(
        "hqk,hqd->hkd", probability.astype(bf16), grad_mixed, preferred_element_type=f32
    )
    grad_prob = jnp.einsum("hqd,hkd->hqk", grad_mixed, value_heads, preferred_element_type=f32)
    row_delta = jnp.sum(probability * grad_prob, axis=-1, keepdims=True)
    grad_scores = (probability * (grad_prob - row_delta)).astype(bf16)
    grad_queries = jnp.einsum(
        "hqk,hkd->hqd", grad_scores, key_heads, preferred_element_type=f32
    ) * HD ** (-0.5)
    grad_key_heads = jnp.einsum(
        "hqk,hqd->hkd", grad_scores, queries, preferred_element_type=f32
    ) * HD ** (-0.5)
    return grad_queries, grad_key_heads, grad_value_heads


def local(
    tokens, doc_lengths, w_query, w_key, w_value, w_out, w_gate, w_up, w_down, norm_gains, cotangent
):
    plan = Plan()
    micro_count, sequences, half_rows, width = tokens.shape
    assert micro_count == 2 and sequences == 1
    quarter = half_rows // 2
    heads = w_query.shape[2] // HD
    n = plan.n
    group = 2 * plan.y + plan.x
    qw, kw = heads * HD, 2 * HD

    kv_at = plan.t * heads // GROUP_SIZE * HD
    hidden_units = w_gate.shape[2]
    attn_width = qw + 2 * kw + qw
    attn_shards = []
    for layer in range(LAYERS):
        keys = lax.dynamic_slice_in_dim(w_key[layer], kv_at, kw, axis=1)
        values = lax.dynamic_slice_in_dim(w_value[layer], kv_at, kw, axis=1)
        attn_shards += [w_query[layer], keys, values, w_out[layer].T]
    swapped = [plan.swap(jnp.concatenate(attn_shards, axis=1))]
    swapped[-1], w_gate, w_up, w_down, tokens, cotangent, norm_gains = lax.optimization_barrier(
        (swapped[-1], w_gate, w_up, w_down, tokens, cotangent, norm_gains)
    )
    for layer in range(LAYERS):
        shard = jnp.concatenate([w_gate[layer], w_up[layer], w_down[layer].T], axis=1)
        if layer:
            shard, swapped[-1] = lax.optimization_barrier((shard, swapped[-1]))
        swapped.append(plan.swap(shard))
    owned = []
    for index, shard in enumerate(swapped):
        if index > 1:
            shard, owned[-1] = lax.optimization_barrier((shard, owned[-1]))
        owned.append(lax.all_gather(shard, "dp", axis=0, tiled=True))

    def columns(halves, start, stop):
        return tuple(part[:, start:stop] for part in halves)

    def both_parities(own, after=None):
        if after is not None:
            own, after = lax.optimization_barrier((own, after))
        return (own, plan.core(own)), after

    side = lax.ppermute(norm_gains, "ctx", [(0, 1), (1, 0)])
    pair = jnp.where(
        plan.x == 0,
        jnp.concatenate([norm_gains, side], axis=1),
        jnp.concatenate([side, norm_gains], axis=1),
    )
    gain_pieces = [pair]
    for _ in range(1, n):
        gain_pieces.append(lax.ppermute(gain_pieces[-1], "dp", plan.down))
    ring = jnp.concatenate(gain_pieces + gain_pieces, axis=1)
    gain_width = pair.shape[1]
    gains = lax.dynamic_slice_in_dim(
        ring, (n - plan.z) % n * gain_width, n * gain_width, axis=1
    ).astype(f32)
    gain_attn = plan.inward(gains[:, :width])
    gain_ffn = plan.inward(gains[:, width : 2 * width])
    gain_query = gains[:, 2 * width : 2 * width + HD]
    gain_key = gains[:, 2 * width + HD :]

    blocks = jnp.arange(4, dtype=jnp.int32) ^ (2 * plan.x + plan.y).astype(jnp.int32)
    places = (blocks[:, None] * quarter + jnp.arange(quarter, dtype=jnp.int32)[None, :]).reshape(-1)
    lengths = lax.dynamic_index_in_dim(doc_lengths, plan.c, axis=0, keepdims=False)[0]
    docs = lengths.shape[0]
    ends = jnp.cumsum(lengths, dtype=jnp.int32)
    starts = ends - lengths
    document = jnp.sum((places[:, None] >= ends[None, :]).astype(jnp.int32), axis=-1)
    chosen = document[:, None] == jnp.arange(docs, dtype=jnp.int32)[None, :]
    position = places - jnp.sum(jnp.where(chosen, starts[None, :], 0), axis=-1)
    segment = jnp.where(document < docs, document, -1)
    allowed = (
        (segment[:, None] == segment[None, :])
        & (segment[:, None] >= 0)
        & (places[None, :] <= places[:, None])
    )[None]
    frequency = rope_base ** (-jnp.arange(HD // 2, dtype=f32) * (2.0 / HD))
    angle = position.astype(f32)[:, None] * frequency
    cosine, sine_value = jnp.cos(angle), jnp.sin(angle)
    pair_start = group * heads // GROUP_SIZE
    first_pair = (
        group * heads + jnp.arange(heads, dtype=jnp.int32)
    ) // GROUP_SIZE == pair_start
    weight_first = first_pair.astype(f32)[:, None, None]

    def own_half(array):
        rows = lax.dynamic_index_in_dim(array, plan.c, axis=0, keepdims=False)[0]
        rows = jnp.where(plan.y == 0, rows, jnp.roll(rows, quarter, axis=0))
        return plan.inward(rows)

    def by_head(array, count):
        return jnp.swapaxes(array.reshape(array.shape[0], count, HD), 0, 1)

    def flat(array):
        return jnp.swapaxes(array, 0, 1).reshape(array.shape[1], -1)

    first_half = own_half(tokens)
    cot_half = own_half(cotangent)
    cot_all = jnp.concatenate([cot_half, plan.peer(cot_half, 2)], axis=0)
    tokens_all = jnp.concatenate([first_half, plan.peer(first_half, 2)], axis=0).astype(f32)
    start_grad = jnp.where(segment[:, None] >= 0, cot_all, jnp.zeros_like(cot_all))

    state = tokens_all[:quarter]
    stored = []
    fetched = []
    attn_all, _ = both_parities(owned[0])
    for layer in range(LAYERS):
        attn_w = columns(attn_all, layer * attn_width, (layer + 1) * attn_width)
        w_qkv = columns(attn_w, 0, qw + 2 * kw)
        w_o = columns(attn_w, qw + 2 * kw, None)
        if layer == 0:
            scale_in = scale_of(tokens_all)
            normed = (tokens_all * scale_in * gain_attn[layer]).astype(bf16)
            normed, start_grad = lax.optimization_barrier((normed, start_grad))
            scale_in = scale_in[:quarter]
        else:
            scale_in = scale_of(state)
            normed = next_normed
        qkv = plan.into(normed, w_qkv)
        queries = by_head(qkv[:, :qw], heads)
        query_scale = scale_of(queries)
        query_low = rotate(queries * query_scale * gain_query[layer], cosine, sine_value).astype(
            bf16
        )
        keys = by_head(qkv[:, qw : qw + kw], 2)
        key_scale = scale_of(keys)
        key_low = rotate(keys * key_scale * gain_key[layer], cosine, sine_value).astype(bf16)
        value_low = by_head(qkv[:, qw + kw :].astype(bf16), 2)
        key_heads = jnp.where(first_pair[:, None, None], key_low[0][None], key_low[1][None])
        value_heads = jnp.where(first_pair[:, None, None], value_low[0][None], value_low[1][None])
        mixed, merged = attend(query_low, key_heads, value_heads, allowed)
        mixed_low = flat(mixed.astype(bf16))
        attn_terms = plan.out_of(mixed_low, w_o)
        middle, normed2 = join(attn_terms, state, gain_ffn[layer])
        ffn_w, later_middle = both_parities(owned[layer + 1], middle)
        w_g = columns(ffn_w, 0, hidden_units)
        w_u = columns(ffn_w, hidden_units, 2 * hidden_units)
        w_gu = columns(ffn_w, 0, 2 * hidden_units)
        scale_mid = scale_of(middle)
        gate = plan.into(normed2, w_g)
        up = plan.into(normed2, w_u)
        hidden = (jax.nn.silu(gate) * up).astype(bf16)
        w_d = columns(ffn_w, 2 * hidden_units, None)
        ffn_terms = plan.out_of(hidden, w_d)
        fetched.append((w_qkv, w_o, w_d, w_gu))
        stored.append(
            (
                state,
                scale_in,
                normed,
                queries,
                query_scale,
                query_low,
                keys,
                key_scale,
                key_heads,
                value_heads,
                merged,
                mixed_low,
                middle,
                scale_mid,
                normed2,
                gate,
                up,
                hidden,
            )
        )
        if layer + 1 < LAYERS:
            state, next_normed = join(ffn_terms, later_middle, gain_attn[layer + 1])

    gradient = start_grad[:quarter].astype(f32)
    grad_ffn = start_grad
    results = [[None] * 3 for _ in range(LAYERS)]
    last = []

    def finish(term):
        moved = plan.swap(term)
        keys = jnp.zeros((term.shape[0], w_key.shape[2]), f32)
        values = keys
        for j in range(plan.nt):
            part = moved[:, qw : qw + 2 * kw] if j == 0 else plan.cross(term[:, qw : qw + 2 * kw], j)
            part = part.astype(f32)
            sender = 2 * (plan.y ^ (j // 2)) + (plan.c ^ (j % 2))
            at = sender * heads // GROUP_SIZE * HD
            zeros = jnp.zeros_like(keys)
            keys += lax.dynamic_update_slice_in_dim(zeros, part[:, :kw], at, axis=1)
            values += lax.dynamic_update_slice_in_dim(zeros, part[:, kw:], at, axis=1)
        query = moved[:, :qw].astype(f32)
        out = moved[:, qw + 2 * kw :].T.astype(f32)
        return query, keys, values, out

    def scatter_next(layer, member, term):
        if len(last) > 1:
            at, part = last[-2]
            term, results[at][part] = lax.optimization_barrier((term, results[at][part]))
        results[layer][member] = plan.scatter(term)
        last.append((layer, member))

    gain_grads = [None] * LAYERS
    for layer in reversed(range(LAYERS)):
        w_qkv, w_o, w_d, w_gu = fetched[layer]
        (
            state,
            scale_in,
            normed,
            queries,
            query_scale,
            query_low,
            keys,
            key_scale,
            key_heads,
            value_heads,
            merged,
            mixed_low,
            middle,
            scale_mid,
            normed2,
            gate,
            up,
            hidden,
        ) = stored[layer]
        if grad_ffn is None:
            grad_ffn, results[layer + 1][1] = plan.spread_beside(
                gradient.astype(bf16), results[layer + 1][1]
            )
        term_d = plan.weight_term(grad_ffn, hidden)
        if layer + 1 == LAYERS:
            scatter_next(layer, 2, term_d)
        grad_hidden = plan.into(grad_ffn, w_d)
        sigmoid_gate = jax.nn.sigmoid(gate)
        grad_gate = (
            grad_hidden * up * sigmoid_gate * (1.0 + gate * (1.0 - sigmoid_gate))
        ).astype(bf16)
        grad_up = (grad_hidden * (gate * sigmoid_gate)).astype(bf16)
        grad_gu = jnp.concatenate([grad_gate, grad_up], axis=1)
        if layer + 1 < LAYERS:
            above = results[layer + 1]
            ffn_high = plan.swap(jnp.concatenate([above[1], above[2]], axis=1))
            grad_gu, ffn_high, term_d = lax.optimization_barrier((grad_gu, ffn_high, term_d))
        term_gu = plan.weight_term(normed2, grad_gu)
        mid_terms = plan.out_of(grad_gu, w_gu)
        if layer + 1 == LAYERS:
            summed_mid, term_gu = plan.gather_sum(mid_terms, term_gu)
        else:
            mid_terms, above[0] = lax.optimization_barrier((mid_terms, above[0]))
            scatter_next(layer, 2, term_d)
            summed_mid, term_gu = plan.gather_sum(mid_terms, term_gu)
            summed_mid, results[layer][2] = lax.optimization_barrier(
                (summed_mid, results[layer][2])
            )
        scatter_next(layer, 1, term_gu)
        grad_g_ffn = jnp.sum(summed_mid * middle * scale_mid, axis=0)
        grad_mid = gradient + norm_back(summed_mid, middle, scale_mid, gain_ffn[layer])
        grad_attn = plan.spread(grad_mid.astype(bf16))
        grad_mixed = by_head(plan.into(grad_attn, w_o).astype(bf16), heads)
        term_o = plan.weight_term(grad_attn, mixed_low)
        grad_query_rot, grad_key_heads, grad_value_heads = attend_back(
            query_low, key_heads, value_heads, grad_mixed, merged, allowed
        )
        grad_key_rot = jnp.stack(
            [
                jnp.sum(grad_key_heads * weight_first, axis=0),
                jnp.sum(grad_key_heads * (1.0 - weight_first), axis=0),
            ]
        )
        grad_values = jnp.concatenate(
            [
                jnp.sum(grad_value_heads * weight_first, axis=0),
                jnp.sum(grad_value_heads * (1.0 - weight_first), axis=0),
            ],
            axis=1,
        ).astype(bf16)
        grad_query_norm = rotate(grad_query_rot, cosine, -sine_value)
        grad_g_query = jnp.sum(grad_query_norm * queries * query_scale, axis=(0, 1))
        grad_queries = flat(
            norm_back(grad_query_norm, queries, query_scale, gain_query[layer]).astype(bf16)
        )
        grad_key_norm = rotate(grad_key_rot, cosine, -sine_value)
        grad_g_key = jnp.sum(grad_key_norm * keys * key_scale, axis=(0, 1))
        grad_keys = flat(norm_back(grad_key_norm, keys, key_scale, gain_key[layer]).astype(bf16))
        grad_qkv = jnp.concatenate([grad_queries, grad_keys, grad_values], axis=1)
        if layer + 1 < LAYERS:
            attn_high = finish(results[layer + 1][0])
            down_low = plan.swap(results[layer][2])
            grad_qkv, attn_high, down_low = lax.optimization_barrier(
                (grad_qkv, attn_high, down_low)
            )
        term_qkv = plan.weight_term(normed, grad_qkv)
        beside = [term_o, term_qkv]
        if layer + 1 < LAYERS:
            downs = [down_low.T, ffn_high[:, 2 * hidden_units :].T]
            beside.append(jnp.stack(downs).astype(f32))
        summed_in, (term_o, term_qkv, *finished) = plan.gather_sum(
            plan.out_of(grad_qkv, w_qkv), beside
        )
        scatter_next(layer, 0, jnp.concatenate([term_qkv, term_o], axis=1))
        grad_g_attn = jnp.sum(summed_in * state * scale_in, axis=0)
        gradient = grad_mid + norm_back(summed_in, state, scale_in, gain_attn[layer])
        grad_ffn = None
        gain_grads[layer] = jnp.concatenate(
            [plan.outward(grad_g_attn), plan.outward(grad_g_ffn), grad_g_query, grad_g_key]
        )
    ffn_terms, gradient = lax.optimization_barrier((ffn_terms, gradient))
    ffn, _ = plan.gather_sum(ffn_terms)
    output = plan.both_quarters(plan.outward((later_middle + ffn).astype(bf16)))
    output = (output, plan.core(output))
    grad_input = plan.both_quarters(plan.outward(gradient.astype(bf16)))
    grad_input = (grad_input, plan.core(grad_input))
    all_gains = plan.total(jnp.stack(gain_grads))

    ffn_low = plan.swap(results[0][1])
    grad_down = finished[0]
    attn_low, ffn_low, grad_down, output, grad_input, all_gains = lax.optimization_barrier(
        (results[0][0], ffn_low, grad_down, output, grad_input, all_gains)
    )
    grad_gate = jnp.stack([ffn[:, :hidden_units] for ffn in (ffn_low, ffn_high)])
    grad_up = jnp.stack([ffn[:, hidden_units : 2 * hidden_units] for ffn in (ffn_low, ffn_high)])
    output = plan.both_micro(*output)
    grad_input = plan.both_micro(*grad_input).astype(f32)
    grad_query, grad_key, grad_value, grad_out = (
        jnp.stack(pair) for pair in zip(finish(attn_low), attn_high)
    )
    share = norm_gains.shape[1]
    grad_gains = lax.dynamic_slice_in_dim(
        all_gains, (2 * plan.z + plan.x) * share, share, axis=1
    )
    return (
        output[:, None],
        grad_input[:, None],
        grad_query,
        grad_key,
        grad_value,
        grad_out,
        grad_gate.astype(f32),
        grad_up.astype(f32),
        grad_down,
        grad_gains,
    )


def solution(mesh):
    placed = (
        P(None, "dp", "ctx", None),
        P(None, "dp", None),
        P(None, ("dp", "ctx"), "tensor"),
        P(None, ("dp", "ctx"), None),
        P(None, ("dp", "ctx"), None),
        P(None, "tensor", ("dp", "ctx")),
        P(None, ("dp", "ctx"), "tensor"),
        P(None, ("dp", "ctx"), "tensor"),
        P(None, "tensor", ("dp", "ctx")),
        P(None, ("dp", "ctx")),
        P(None, "dp", "ctx", None),
    )
    return jax.shard_map(
        local,
        mesh=mesh,
        in_specs=placed,
        out_specs=(
            P(None, "dp", "ctx", None),
            P(None, "dp", "ctx", None),
            P(None, ("dp", "ctx"), "tensor"),
            P(None, ("dp", "ctx"), None),
            P(None, ("dp", "ctx"), None),
            P(None, "tensor", ("dp", "ctx")),
            P(None, ("dp", "ctx"), "tensor"),
            P(None, ("dp", "ctx"), "tensor"),
            P(None, "tensor", ("dp", "ctx")),
            P(None, ("dp", "ctx")),
        ),
        check_vma=False,
    )
```
